32 devices in a mesh: groups: 2 (over y), tx: 4 (over z), ty: 2 (over x), sl: 2 (over core).
Axes of the slice: x: 2, y: 2, z: 4, core: 2. Of those that a mesh axis runs over, the one named last changes fastest.
Arguments:
- object_field: float32 [8, 2, 1024, 1024], P(('groups', 'sl'), None, 'tx', 'ty'), parts along dimension 0, may hold values from -1 to 2
- probe_wave: float32 [4, 128, 128], P('groups'), parts along dimension 0, may hold values from -4.2 to 4.2
- measured: float32 [96, 128, 128], P(('groups', 'tx', 'ty')), parts along dimension 0, may hold values from 0.1 to 4
- owner_row: int32 [96, 1], P(('groups', 'tx', 'ty')), parts along dimension 0, may hold values from 0 to 3; in each aligned block of 6 rows (0 to 5, 6 to 11, ...) at most 3 rows name the same one
- list_rows: int32 [8, 2, 4, 3], P(('groups', 'tx'), 'ty'), parts along dimension 0, may hold values from 0 to 128
- list_cols: int32 [8, 2, 4, 3], P(('groups', 'tx'), 'ty'), parts along dimension 0, may hold values from 0 to 384
Outputs:
- object_out: float32 [8, 2, 1024, 1024], P(('groups', 'sl'), None, 'tx', 'ty'), parts along dimension 0
- probe_out: float32 [4, 128, 128], P('groups'), parts along dimension 0
The draws below stay inside these ranges and needn't reach their ends.
There are 2 independent parts, one for each index of `groups`. The reference program is written for one: setup_inputs(seed, part) draws one part's arguments, and reference() takes and returns one part's arrays. A program takes and returns all parts, laid end to end along the dimension named above; each array names one. Nothing has to cross between parts.
Inputs may be any that keep to these rules, and one draw needn't show every extreme that they name: `owner_row`: at most 3 positions of the rows of one device name the same tile row, and some device reaches 3. `list_rows`: entry [o, j, s, k] belongs to the k-th position (in order) of device (s, j) whose tile row is o; entries with k at or past that device's count for o are not read. Every window lies inside one tile. `list_cols`: same order as list_rows.
All inputs are finite; a program needn't handle non-finite values.
Results may differ from the reference program's by a relative error of at most 0.0098.
Values may be sent and summed in bfloat16 or wider, within the bound.
A program may use at most 192 MiB of HBM per device.

```python
import math
import jax
import jax.numpy as jnp
import numpy as np
from jax import lax

PW = 128
ITERS = 2
TR = 256
TC = 512
POS_DEV = 6
SLICES = 4
NR = 1024
NC = 1024
NPOS = 48
CAP = 3
N_TX = 4
N_TY = 2


def draw_object_field(key, part):
    shape = (SLICES, 2, NR, NC)
    noise = jnp.clip(jax.random.normal(key, shape, jnp.float32), -4.0, 4.0)
    center = jnp.where(jnp.arange(2) == 0, 1.0, 0.0).astype(jnp.float32).reshape(1, 2, 1, 1)
    return center + 0.25 * noise


def set_ends(entries, own_key, smallest, top_value):
    extent = entries.shape
    spot = [jax.random.randint(jax.random.fold_in(own_key, axis), (), 0, extent[axis]) for axis in range(len(extent))]
    entries = entries.at[tuple(spot)].set(smallest)
    longest = extent.index(max(extent))
    spot[longest] = (spot[longest] + 1) % extent[longest]
    return entries.at[tuple(spot)].set(top_value)


def block_levels(key, extent, cuts, least, largest):
    loudness, own = 1.0, jax.random.fold_in(key, 6)
    for axis_at, parts in cuts:
        draws = jnp.exp(jax.random.uniform(jax.random.fold_in(own, axis_at), (parts,), jnp.float32, least / len(cuts), largest / len(cuts)))
        loudness = loudness * jnp.repeat(draws, extent[axis_at] // parts).reshape([-1 if axis == axis_at else 1 for axis in range(len(extent))])
    return loudness


def routed_block(stream_key, own, number, rows, amount, top, reach, slope):
    ranking = jax.random.permutation(stream_key, amount)
    packed, common = portions_of(amount, rows * top, reach, slope, True), portions_of(amount, rows * top, reach, slope, False)
    places = jnp.arange(amount)

    def named(sizes, turn):
        used = int((sizes > 0).sum())
        fixed = max(1, used // 4)
        shifted = fixed + (places - fixed + turn * (used - fixed)) % max(1, amount - fixed)
        return jnp.zeros((amount,), jnp.int32).at[ranking[jnp.where(places < fixed, places, shifted)]].set(jnp.asarray(sizes, jnp.int32))

    sizes = jnp.where(number % 4 == 0, named(packed, number // 4), named(common, number - number // 4 - 1))
    mixed = jax.random.permutation(jax.random.fold_in(own, 3), amount)
    source_of, taker = mixed[0:amount // 2 * 2:2], mixed[1:amount // 2 * 2:2]
    margin = jnp.minimum(sizes[source_of] - 1, reach - sizes[taker]) // 2
    margin = jnp.where((source_of == ranking[0]) | (taker == ranking[0]) | (sizes[taker] == 0), 0, jnp.maximum(margin, 0))
    shifted = jax.random.randint(jax.random.fold_in(own, 4), (amount // 2,), 0, 1 << 20) % (margin + 1)
    sizes = sizes.at[source_of].add(-shifted).at[taker].add(shifted)
    items = jnp.searchsorted(jnp.cumsum(sizes), jnp.arange(rows * top), side="right").astype(jnp.int32)
    grid = items.reshape(top, rows).T
    grid = grid[jax.random.permutation(jax.random.fold_in(own, 1), rows)]
    turn = jax.random.randint(jax.random.fold_in(own, 2), (rows, 1), 0, top)
    return jnp.take_along_axis(grid, (jnp.arange(top)[None, :] + turn) % top, axis=1)


def portions_of(amount, total, limit, skew, full):
    loads = [(1 << 20) // math.isqrt(grade ** skew) + 1 for grade in range(1, amount + 1)]
    largest = limit if full else min(limit, max(-(-total // amount), total * loads[0] // sum(loads)))
    least = 1 if total - largest >= amount - 1 else 0
    holding, rest = [largest] + [least] * (amount - 1), total - largest - least * (amount - 1)
    while rest > 0:
        candidates = [i for i in range(1, amount) if holding[i] < largest] or [i for i in range(1, amount) if holding[i] < limit]
        pool, budget = sum([loads[i] for i in candidates]), rest
        for i in candidates:
            addition = min(limit - holding[i], max(1, budget * loads[i] // pool), rest)
            holding[i] = holding[i] + addition
            rest = rest - addition
    return np.array(holding)


def centred(stream_key, extent, width, bound, kind=jnp.bfloat16):
    entries = jax.random.normal(stream_key, extent, jnp.float32) * width
    return jnp.minimum(jnp.maximum(entries, -bound), bound).astype(kind)


def setup_inputs(seed: int = 0, part: int = 0) -> dict:
    keys = jax.random.split(jax.random.key(seed), 7)
    part_splits = jax.random.split(jax.random.fold_in(keys[6], part), 7)
    object_field = draw_object_field(jax.random.fold_in(jax.random.fold_in(keys[6], part), 71), part)
    probe_wave = centred(part_splits[1], (2, PW, PW), 0.7, 4.2, jnp.float32)
    measured = jnp.clip(jnp.exp(math.log(4.0) - 3.6888794 * jax.random.uniform(part_splits[2], (NPOS, PW, PW), jnp.float32) ** block_levels(part_splits[2], (NPOS, PW, PW), ((0, 8),), -0.2, 0.2)), 0.1, 4.0)
    owner_row_keys = jax.random.split(jax.random.fold_in(part_splits[3], 1), NPOS // POS_DEV)
    owner_row_turns = jax.random.permutation(jax.random.fold_in(part_splits[3], 3), NPOS // POS_DEV)
    owner_row = jax.vmap(lambda own, number: routed_block(jax.random.fold_in(part_splits[3], 2), own, number, POS_DEV, N_TX, 1, CAP, 2))(owner_row_keys, owner_row_turns).reshape((NPOS, 1))
    list_rows = set_ends(jax.random.randint(part_splits[4], (N_TX, N_TY, N_TX, CAP), 0, TR - PW + 1), jax.random.fold_in(part_splits[4], 1), 0, TR - PW).astype(jnp.int32)
    list_cols = set_ends(jax.random.randint(part_splits[5], (N_TX, N_TY, N_TX, CAP), 0, TC - PW + 1), jax.random.fold_in(part_splits[5], 1), 0, TC - PW).astype(jnp.int32)
    return {"object_field": object_field, "probe_wave": probe_wave, "measured": measured, "owner_row": owner_row, "list_rows": list_rows, "list_cols": list_cols}


PHASE = 0.25
STEP_OBJECT = 0.01
STEP_PROBE = 0.6
precise = lax.Precision.HIGHEST

def make_tables(pixels):
    indices = jnp.arange(pixels, dtype=jnp.int32)
    modulus = indices[:, None] * indices[None, :] % pixels
    angles = modulus.astype(jnp.float32) * (2.0 * math.pi / pixels)
    norm_factor = 1.0 / math.sqrt(pixels)
    four_re = jnp.cos(angles) * norm_factor
    four_im = -jnp.sin(angles) * norm_factor
    frequency = jnp.where(indices < pixels // 2, indices, indices - pixels).astype(jnp.float32)
    phases = PHASE * frequency * frequency / pixels
    filter_re = jnp.cos(phases)
    filter_im = -jnp.sin(phases)
    left_re = four_re * filter_re[None, :] + four_im * filter_im[None, :]
    left_im = four_re * filter_im[None, :] - four_im * filter_re[None, :]
    kern_re = jnp.dot(left_re, four_re, precision=precise) - jnp.dot(left_im, four_im, precision=precise)
    kern_im = jnp.dot(left_re, four_im, precision=precise) + jnp.dot(left_im, four_re, precision=precise)
    return (kern_re, kern_im, four_re, four_im)

def mult_left(matrix, values):
    return jnp.einsum('ij,bjk->bik', matrix, values, precision=precise)

def mult_right(values, matrix):
    return jnp.einsum('bij,kj->bik', values, matrix, precision=precise)

def apply_both(mat_re, mat_im, wave_re, wave_im):
    mid_re = mult_left(mat_re, wave_re) - mult_left(mat_im, wave_im)
    mid_im = mult_left(mat_re, wave_im) + mult_left(mat_im, wave_re)
    out_re = mult_right(mid_re, mat_re) - mult_right(mid_im, mat_im)
    out_im = mult_right(mid_re, mat_im) + mult_right(mid_im, mat_re)
    return (out_re, out_im)

def wave_times(a_re, a_im, b_re, b_im):
    return (a_re * b_re - a_im * b_im, a_re * b_im + a_im * b_re)

def position_misfit(patch, probe_in, pattern, tables):
    kern_re, kern_im, four_re, four_im = tables
    wave_re, wave_im = wave_times(probe_in[0][None], probe_in[1][None], patch[None, 0, 0], patch[None, 0, 1])
    for layer in range(1, SLICES):
        wave_re, wave_im = apply_both(kern_re, kern_im, wave_re, wave_im)
        wave_re, wave_im = wave_times(wave_re, wave_im, patch[None, layer, 0], patch[None, layer, 1])
    far_re, far_im = apply_both(four_re, four_im, wave_re, wave_im)
    misfit = far_re * far_re + far_im * far_im - pattern[None]
    return 0.5 * jnp.sum(misfit * misfit)

def reference(object_field, probe_wave, measured, owner_row, list_rows, list_cols):
    tables = make_tables(PW)
    device_of = jnp.arange(NPOS, dtype=jnp.int32) // POS_DEV
    source_row = device_of // N_TY
    col_tile = device_of % N_TY
    owner_of = owner_row[:, 0].astype(jnp.int32)
    blocks = owner_of.reshape(N_TX * N_TY, POS_DEV)
    order_ids = jnp.arange(POS_DEV, dtype=jnp.int32)
    earlier = order_ids[None, :] < order_ids[:, None]
    same = blocks[:, :, None] == blocks[:, None, :]
    bucket_rank = lax.optimization_barrier(jnp.sum(jnp.where(same & earlier[None], 1, 0), axis=2)).reshape(NPOS).astype(jnp.int32)
    row_at = (owner_of * TR + list_rows[owner_of, col_tile, source_row, bucket_rank]).astype(jnp.int32)
    col_at = (col_tile * TC + list_cols[owner_of, col_tile, source_row, bucket_rank]).astype(jnp.int32)
    anchor = jnp.zeros((), jnp.int32)
    field_now = object_field
    wave_now = probe_wave
    for sweep in range(ITERS):

        def visit_one(carry, entry):
            grad_sum, probe_sum = carry
            row_one, col_one, pattern = entry
            corner = (anchor, anchor, row_one, col_one)
            patch = lax.dynamic_slice(field_now, corner, (SLICES, 2, PW, PW))
            patch = lax.optimization_barrier(patch.astype(jnp.bfloat16)).astype(jnp.float32)
            grad_patch, grad_probe = jax.grad(position_misfit, argnums=(0, 1))(patch, wave_now, pattern, tables)
            grad_patch = lax.optimization_barrier(grad_patch.astype(jnp.bfloat16)).astype(jnp.float32)
            before = lax.dynamic_slice(grad_sum, corner, (SLICES, 2, PW, PW))
            grad_sum = lax.dynamic_update_slice(grad_sum, before + grad_patch, corner)
            return ((grad_sum, probe_sum + grad_probe), None)
        start = (jnp.zeros(field_now.shape, jnp.float32), jnp.zeros(wave_now.shape, jnp.float32))
        (grad_sum, probe_sum), unused = lax.scan(visit_one, start, (row_at, col_at, measured))
        field_now = field_now - STEP_OBJECT * grad_sum
        wave_now = wave_now - STEP_PROBE / NPOS * probe_sum
    return (field_now, wave_now)
```

```python
import functools
import math

import jax
import jax.numpy as jnp
import numpy as np
from jax import lax
from jax.experimental import pallas as pl
from jax.experimental.pallas import tpu as pltpu
from jax.sharding import PartitionSpec as P

ITERS = 2
PHASE = 0.25
STEP_OBJECT = 0.01
STEP_PROBE = 0.6
F32 = jnp.float32
BF16 = jnp.bfloat16
MESH = pl.DeviceIdType.MESH


def real_tables(pixels):
    index = np.arange(pixels)
    four = np.exp(-2j * math.pi * ((index[:, None] * index[None, :]) % pixels) / pixels) / math.sqrt(pixels)
    freq = np.where(index < pixels // 2, index, index - pixels).astype(np.float64)
    kern = (np.conj(four) * np.exp(-1j * PHASE * freq * freq / pixels)[None, :]) @ four
    found = []
    for matrix in (kern, four):
        right = np.block([[matrix.real, matrix.imag], [-matrix.imag, matrix.real]])
        found += [right, right.T]
    whole = np.stack(found).astype(np.float32)
    high = whole.astype(jnp.bfloat16)
    low = (whole - high.astype(np.float32)).astype(jnp.bfloat16)
    return np.stack([high, low], axis=1)


def split(x):
    high = x.astype(BF16)
    return high, (x - high.astype(F32)).astype(BF16)


def dot(a, b):
    return jnp.dot(a, b, preferred_element_type=F32)


def loop(count, step):
    if count <= 8:
        for i in range(count):
            step(i)
    else:
        lax.fori_loop(0, count, lambda i, carry: (step(i), carry)[1], 0)


def lanes(i, width):
    return pl.ds(i * width if isinstance(i, int) else pl.multiple_of(i * width, width), width)


def both_sides(x, tabs, right, left, px, fine=True):
    count = x.shape[1] // px

    def rows(v):
        return jnp.concatenate(
            [
                jnp.concatenate([v[:px, s * px : (s + 1) * px], v[px:, s * px : (s + 1) * px]], axis=1)
                for s in range(count)
            ],
            axis=0,
        )

    def columns(v):
        return jnp.concatenate(
            [
                jnp.concatenate([v[s * px : (s + 1) * px, :px], v[s * px : (s + 1) * px, px:]], axis=0)
                for s in range(count)
            ],
            axis=1,
        )

    m_high, m_low = tabs[right, 0], tabs[right, 1]
    if not fine:
        v = rows(x.astype(BF16))
        y = dot(jnp.concatenate([v, v], axis=1), jnp.concatenate([m_high, m_low], axis=0))
        v = columns(y.astype(BF16))
        m_high, m_low = tabs[left, 0], tabs[left, 1]
        return dot(jnp.concatenate([m_high, m_low], axis=1), jnp.concatenate([v, v], axis=0))
    high, low = split(x)
    high, low = rows(high), rows(low)
    y = dot(
        jnp.concatenate([high, low, high], axis=1), jnp.concatenate([m_high, m_high, m_low], axis=0)
    )
    high, low = split(y)
    high, low = columns(high), columns(low)
    m_high, m_low = tabs[left, 0], tabs[left, 1]
    return dot(
        jnp.concatenate([m_high, m_high, m_low], axis=1), jnp.concatenate([high, low, high], axis=0)
    )


def times(a, b, px):
    ar, ai, br, bi = a[:px], a[px:], b[:px], b[px:]
    return jnp.concatenate([ar * br - ai * bi, ar * bi + ai * br], axis=0)


def conj_times(a, g, px):
    ar, ai, gr, gi = a[:px], a[px:], g[:px], g[px:]
    return jnp.concatenate([ar * gr + ai * gi, ar * gi - ai * gr], axis=0)


def kernel(
    n_tx, n_ty, n_sl, cap, all_positions,
    obj, probe, measured, list_r, list_c, owner, tabs,
    obj_out, probe_out,
    tile, pat, staged, cut_r, cut_c, put_r, put_c, patches, phis, grads, g_recv, placed,
    pieces, pg_mine, delta_mine, deltas, wave, pg_sum,
    tile_send, tile_recv, pat_send, pat_recv, g_send, g_rcv, pc_send, pc_recv, dl_send, dl_recv,
):
    ix, iy, core = lax.axis_index("tx"), lax.axis_index("ty"), lax.axis_index("sl")
    layers, _, rows, cols = obj.shape
    positions, px, _ = measured.shape
    half = n_tx // n_sl
    slots = half * cap
    total = n_sl * layers
    other = 1 - core
    devices = n_tx * n_ty * n_sl
    me = (ix * n_ty + iy) * n_sl + core
    peer = {"sl": other}

    def at(i):
        return {"tx": i // (n_ty * n_sl), "ty": (i // n_sl) % n_ty, "sl": i % n_sl}

    barrier = pltpu.get_barrier_semaphore()

    def greet(i, carry):
        @pl.when(i != me)
        def _():
            pl.semaphore_signal(barrier, inc=1, device_id=at(i), device_id_type=MESH)

        return carry

    lax.fori_loop(0, devices, greet, 0)

    for l in range(layers):
        for part in range(2):
            tile[0, core * layers + l, part] = obj[l, part].astype(BF16)
    wave[...] = jnp.concatenate([probe[0], probe[1]], axis=0)

    def stage(o, carry):
        seen = jnp.int32(0)
        found = [jnp.int32(-1)] * cap
        for p in range(positions):
            here = owner[0, p] == o
            for k in range(cap):
                found[k] = jnp.where(here & (seen == k), jnp.int32(p), found[k])
            seen = seen + jnp.where(here, 1, 0)
        for k in range(cap):
            values = jnp.full((px, px), -1.0, F32)
            for p in range(positions):
                values = jnp.where(found[k] == p, measured[p], values)
            staged[o, k] = values.astype(BF16)
        return carry

    lax.fori_loop(0, n_tx, stage, 0)
    pl.semaphore_wait(barrier, devices - 1)

    def send_tile(it, l):
        where = tile.at[it, core * layers + l]
        copy = pltpu.make_async_remote_copy(
            src_ref=where, dst_ref=where, send_sem=tile_send.at[it, l], recv_sem=tile_recv.at[it, l],
            device_id=peer, device_id_type=MESH,
        )
        copy.start()

    def tile_copy(it, l):
        where = tile.at[it, other * layers + l]
        return pltpu.make_async_remote_copy(
            src_ref=where, dst_ref=where, send_sem=tile_send.at[it, l], recv_sem=tile_recv.at[it, l],
            device_id=peer, device_id_type=MESH,
        )

    for l in range(layers):
        send_tile(0, l)

    mine_sends = (ix // half) == core
    local_s = lax.rem(ix, half)

    def pattern_copy(o, s):
        return pltpu.make_async_remote_copy(
            src_ref=staged.at[o], dst_ref=pat.at[s], send_sem=pat_send.at[o], recv_sem=pat_recv.at[s],
            device_id={"tx": o}, device_id_type=MESH,
        )

    @pl.when(mine_sends)
    def _():
        def send(o, carry):
            @pl.when(o != ix)
            def _():
                pattern_copy(o, local_s).start()

            return carry

        lax.fori_loop(0, n_tx, send, 0)
        pat[local_s] = staged[ix]

    def slot_corner(t, c):
        s, k = c * half + t // cap, t % cap
        return list_r[k, 0, s], list_c[k, 0, s]

    def hot(shape, axis, shift):
        long = lax.broadcasted_iota(jnp.int32, shape, axis)
        short = lax.broadcasted_iota(jnp.int32, shape, 1 - axis)
        return jnp.where(long - short == shift, 1.0, 0.0).astype(BF16)

    def build(t):
        row, col = slot_corner(t, core)
        cut_r[t] = hot((px, rows), 1, row)
        cut_c[:, lanes(t, px)] = hot((cols, px), 0, col)
        put_r[t] = hot((rows, px), 0, row)
        put_c[lanes(t, px), :] = hot((px, cols), 1, col)
        row, col = slot_corner(t, other)
        put_r[slots + t] = hot((rows, px), 0, row)
        put_c[lanes(slots + t, px), :] = hot((px, cols), 1, col)

    loop(slots, build)

    group = 2 if slots % 2 == 0 else 1
    chunk = max(d for d in range(1, 7) if slots % d == 0)
    fine_chunk = 2 if chunk % 2 == 0 else 1
    width = fine_chunk * px

    for it in range(ITERS):
        def cut(pair, start):
            held = tile[it, pl.ds(start, layers)].reshape(layers * 2 * rows, cols)
            narrow = dot(held, cut_c[:, lanes(pair, group * px)]).astype(BF16)
            for i in range(group):
                t = pair * group + i
                wide = jnp.concatenate(
                    [narrow[q * rows : (q + 1) * rows, i * px : (i + 1) * px] for q in range(2 * layers)], axis=1
                )
                done = dot(cut_r[t], wide).astype(BF16)
                for q in range(2 * layers):
                    patches[start + q // 2, q % 2 * px : (q % 2 + 1) * px, lanes(t, px)] = (
                        done[:, q * px : (q + 1) * px]
                    )

        loop(slots // group, lambda pair: cut(pair, core * layers))
        for l in range(layers):
            tile_copy(it, l).wait_recv()
        loop(slots // group, lambda pair: cut(pair, other * layers))

        if it > 0:
            finish_probe(it - 1)

        if it == 0:

            def arrive(i, carry):
                @pl.when(core * half + i != ix)
                def _():
                    pattern_copy(ix, i).wait_recv()

                return carry

            lax.fori_loop(0, half, arrive, 0)

        pg_sum[...] = jnp.zeros_like(pg_sum)

        def run(k):
            first = k * chunk
            spans = [lanes(first // fine_chunk + i, width) for i in range(chunk // fine_chunk)]
            w = jnp.concatenate([wave[...]] * fine_chunk, axis=1)
            psi = [times(w, patches[0, :, span].astype(F32), px) for span in spans]
            for l in range(1, total):
                for i, span in enumerate(spans):
                    phi = both_sides(psi[i], tabs, 0, 1, px)
                    phis[l - 1, :, span] = phi
                    psi[i] = times(phi, patches[l, :, span].astype(F32), px)
            g = []
            for i in range(len(spans)):
                far = both_sides(psi[i], tabs, 2, 3, px)
                target = []
                for s in range(fine_chunk):
                    t = first + i * fine_chunk + s
                    target.append(pat[t // cap, t % cap].astype(F32))
                target = jnp.concatenate(target, axis=1)
                fr, fi = far[:px], far[px:]
                miss = jnp.where(target >= 0.0, 2.0 * (fr * fr + fi * fi - target), 0.0)
                g.append(jnp.concatenate([miss * fr, miss * fi], axis=0))
            g = [both_sides(one, tabs, 3, 2, px, fine=False) for one in g]
            for l in range(total - 1, -1, -1):
                for i, span in enumerate(spans):
                    before = phis[l - 1, :, span] if l else w
                    grads[l, :, span] = conj_times(before, g[i], px).astype(BF16)
                    g[i] = conj_times(patches[l, :, span].astype(F32), g[i], px)
                    if l:
                        g[i] = both_sides(g[i], tabs, 1, 0, px, fine=False)
            for one in g:
                for s in range(fine_chunk):
                    pg_sum[...] += one[:, s * px : (s + 1) * px]

        loop(slots // chunk, run)

        def grad_copy(it):
            return pltpu.make_async_remote_copy(
                src_ref=grads.at[pl.ds(other * layers, layers)], dst_ref=g_recv.at[it],
                send_sem=g_send.at[it], recv_sem=g_rcv.at[it], device_id=peer, device_id_type=MESH,
            )

        grad_copy(it).start()
        pg_mine[it] = pg_sum[...].astype(BF16)
        reducers = delta_count(devices, 2 * px)
        deep = 2 * px // reducers

        def piece_copy(it, i, source):
            return pltpu.make_async_remote_copy(
                src_ref=pg_mine.at[it, pl.ds(pl.multiple_of(i * deep, deep), deep)],
                dst_ref=pieces.at[it, source], send_sem=pc_send.at[it, i], recv_sem=pc_recv.at[it, source],
                device_id=at(i), device_id_type=MESH,
            )

        def send_piece(i, carry):
            @pl.when(i != me)
            def _():
                piece_copy(it, i, me).start()

            return carry

        lax.fori_loop(0, reducers, send_piece, 0)

        def spread(t, values):
            placed_now = dot(put_r[t], values).astype(BF16)
            for q in range(2 * layers):
                placed[q, :, lanes(t, px)] = placed_now[:, q * px : (q + 1) * px]

        def spread_own(t):
            spread(t, jnp.concatenate(
                [grads[core * layers + q // 2, q % 2 * px : (q % 2 + 1) * px, lanes(t, px)]
                 for q in range(2 * layers)], axis=1))

        def spread_got(t):
            spread(slots + t, jnp.concatenate(
                [g_recv[it, q // 2, q % 2 * px : (q % 2 + 1) * px, lanes(t, px)]
                 for q in range(2 * layers)], axis=1))

        loop(slots, spread_own)

        def delta_copy(it, i, source):
            where = pl.ds(pl.multiple_of(source * deep, deep), deep)
            return pltpu.make_async_remote_copy(
                src_ref=delta_mine.at[it], dst_ref=deltas.at[it, where],
                send_sem=dl_send.at[it, i], recv_sem=dl_recv.at[it, source],
                device_id=at(i), device_id_type=MESH,
            )

        @pl.when(me < reducers)
        def _():
            own = pl.ds(pl.multiple_of(me * deep, deep), deep)
            pieces[it, me] = pg_mine[it, own]

            def wait_piece(i, carry):
                @pl.when(i != me)
                def _():
                    piece_copy(it, me, i).wait_recv()

                return carry

            lax.fori_loop(0, devices, wait_piece, 0)
            add = lax.fori_loop(
                0, devices, lambda i, acc: acc + pieces[it, i].astype(F32), jnp.zeros((deep, px), F32)
            )
            delta_mine[it] = add.astype(BF16)
            deltas[it, own] = delta_mine[it]

            def send_delta(i, carry):
                @pl.when(i != me)
                def _():
                    delta_copy(it, i, me).start()

                return carry

            lax.fori_loop(0, devices, send_delta, 0)

        def finish_probe(it):
            def wait_delta(i, carry):
                @pl.when(i != me)
                def _():
                    delta_copy(it, me, i).wait_recv()

                return carry

            lax.fori_loop(0, reducers, wait_delta, 0)
            wave[...] -= (STEP_PROBE / all_positions) * deltas[it].astype(F32)

        grad_copy(it).wait_recv()
        loop(slots, spread_got)
        for q in range(2 * layers):
            l, part = q // 2, q % 2
            before = obj[l, part] if it == 0 else obj_out[l, part]
            now = before - STEP_OBJECT * dot(placed[q], put_c[...])
            obj_out[l, part] = now
            if it < ITERS - 1:
                tile[it + 1, core * layers + l, part] = now.astype(BF16)
                if part == 1:
                    send_tile(it + 1, l)
        grad_copy(it).wait_send()

    finish_probe(ITERS - 1)
    probe_out[0] = wave[:px]
    probe_out[1] = wave[px:]

    @pl.when(mine_sends)
    def _():
        def sent(o, carry):
            @pl.when(o != ix)
            def _():
                pattern_copy(o, local_s).wait_send()

            return carry

        lax.fori_loop(0, n_tx, sent, 0)

    for it in range(ITERS):
        for l in range(layers):
            tile_copy(it, l).wait_send()

        def sent_piece(i, carry):
            @pl.when(i != me)
            def _():
                piece_copy(it, i, me).wait_send()

            return carry

        lax.fori_loop(0, reducers, sent_piece, 0)

        @pl.when(me < reducers)
        def _():
            def sent_delta(i, carry):
                @pl.when(i != me)
                def _():
                    delta_copy(it, i, me).wait_send()

                return carry

            lax.fori_loop(0, devices, sent_delta, 0)


def delta_count(devices, rows):
    return min(devices, rows // 16)


def body(object_field, probe_wave, measured, owner_row, list_rows, list_cols):
    layers, _, rows, cols = object_field.shape
    positions, px, _ = measured.shape
    n_tx, n_ty, n_sl = lax.axis_size("tx"), lax.axis_size("ty"), lax.axis_size("sl")
    cap = list_rows.shape[-1]
    half = n_tx // n_sl
    slots = half * cap
    total = n_sl * layers
    devices = n_tx * n_ty * n_sl
    deep = 2 * px // delta_count(devices, 2 * px)
    tabs = jnp.asarray(real_tables(px))
    tables = [jnp.transpose(one, (0, 3, 1, 2)).reshape(cap, 1, n_tx) for one in (list_rows, list_cols)]
    vmem = pl.BlockSpec(memory_space=pltpu.VMEM)
    smem = pl.BlockSpec(memory_space=pltpu.SMEM)
    dma = pltpu.SemaphoreType.DMA
    return pl.pallas_call(
        functools.partial(kernel, n_tx, n_ty, n_sl, cap, positions * n_tx * n_ty),
        out_shape=(
            pltpu.VMEM(object_field.shape, F32),
            pltpu.VMEM(probe_wave.shape, F32),
        ),
        in_specs=[vmem, vmem, vmem, smem, smem, smem, vmem],
        out_specs=(vmem, vmem),
        scratch_shapes=[
            pltpu.VMEM((ITERS, total, 2, rows, cols), BF16),
            pltpu.VMEM((half, cap, px, px), BF16),
            pltpu.VMEM((n_tx, cap, px, px), BF16),
            pltpu.VMEM((slots, px, rows), BF16),
            pltpu.VMEM((cols, slots * px), BF16),
            pltpu.VMEM((2 * slots, rows, px), BF16),
            pltpu.VMEM((2 * slots * px, cols), BF16),
            pltpu.VMEM((total, 2 * px, slots * px), BF16),
            pltpu.VMEM((total - 1, 2 * px, slots * px), F32),
            pltpu.VMEM((total, 2 * px, slots * px), BF16),
            pltpu.VMEM((ITERS, layers, 2 * px, slots * px), BF16),
            pltpu.VMEM((2 * layers, rows, 2 * slots * px), BF16),
            pltpu.VMEM((ITERS, devices, deep, px), BF16),
            pltpu.VMEM((ITERS, 2 * px, px), BF16),
            pltpu.VMEM((ITERS, deep, px), BF16),
            pltpu.VMEM((ITERS, 2 * px, px), BF16),
            pltpu.VMEM((2 * px, px), F32),
            pltpu.VMEM((2 * px, px), F32),
            dma((ITERS, layers)),
            dma((ITERS, layers)),
            dma((n_tx,)),
            dma((half,)),
            dma((ITERS,)),
            dma((ITERS,)),
            dma((ITERS, devices)),
            dma((ITERS, devices)),
            dma((ITERS, devices)),
            dma((ITERS, devices)),
        ],
        compiler_params=pltpu.CompilerParams(
            collective_id=0, has_side_effects=True, vmem_limit_bytes=58 * 2**20
        ),
    )(object_field, probe_wave, measured, *tables, owner_row.reshape(1, -1), tabs)


def solution(mesh):
    in_specs = (
        P(("groups", "sl"), None, "tx", "ty"),
        P("groups", None, None),
        P(("groups", "tx", "ty"), None, None),
        P(("groups", "tx", "ty"), None),
        P(("groups", "tx"), "ty", None, None),
        P(("groups", "tx"), "ty", None, None),
    )
    out_specs = (P(("groups", "sl"), None, "tx", "ty"), P("groups", None, None))
    return jax.shard_map(body, mesh=mesh, in_specs=in_specs, out_specs=out_specs, check_vma=False)
```

```python
import functools
import math

import jax
import jax.numpy as jnp
import numpy as np
from jax import lax
from jax.experimental import pallas as pl
from jax.experimental.pallas import tpu as pltpu
from jax.sharding import PartitionSpec as P

ITERS = 2
PHASE = 0.25
STEP_OBJECT = 0.01
STEP_PROBE = 0.6
F32 = jnp.float32
BF16 = jnp.bfloat16
MESH = pl.DeviceIdType.MESH


def real_tables(pixels):
    index = np.arange(pixels)
    four = np.exp(-2j * math.pi * ((index[:, None] * index[None, :]) % pixels) / pixels) / math.sqrt(pixels)
    freq = np.where(index < pixels // 2, index, index - pixels).astype(np.float64)
    kern = (np.conj(four) * np.exp(-1j * PHASE * freq * freq / pixels)[None, :]) @ four
    found = []
    for matrix in (kern, four):
        right = np.block([[matrix.real, matrix.imag], [-matrix.imag, matrix.real]])
        found += [right, right.T]
    whole = np.stack(found).astype(np.float32)
    high = whole.astype(jnp.bfloat16)
    low = (whole - high.astype(np.float32)).astype(jnp.bfloat16)
    return np.stack([high, low], axis=1)


def split(x):
    high = x.astype(BF16)
    return high, (x - high.astype(F32)).astype(BF16)


def dot(a, b):
    return jnp.dot(a, b, preferred_element_type=F32)


def loop(count, step):
    if count <= 8:
        for i in range(count):
            step(i)
    else:
        lax.fori_loop(0, count, lambda i, carry: (step(i), carry)[1], 0)


def lanes(i, width):
    return pl.ds(i * width if isinstance(i, int) else pl.multiple_of(i * width, width), width)


def both_sides(x, tabs, right, left, px, fine=True):
    count = x.shape[1] // px

    def rows(v):
        return jnp.concatenate(
            [
                jnp.concatenate([v[:px, s * px : (s + 1) * px], v[px:, s * px : (s + 1) * px]], axis=1)
                for s in range(count)
            ],
            axis=0,
        )

    def columns(v):
        return jnp.concatenate(
            [
                jnp.concatenate([v[s * px : (s + 1) * px, :px], v[s * px : (s + 1) * px, px:]], axis=0)
                for s in range(count)
            ],
            axis=1,
        )

    m_high, m_low = tabs[right, 0], tabs[right, 1]
    if not fine:
        v = rows(x.astype(BF16))
        y = dot(jnp.concatenate([v, v], axis=1), jnp.concatenate([m_high, m_low], axis=0))
        v = columns(y.astype(BF16))
        m_high, m_low = tabs[left, 0], tabs[left, 1]
        return dot(jnp.concatenate([m_high, m_low], axis=1), jnp.concatenate([v, v], axis=0))
    high, low = split(x)
    high, low = rows(high), rows(low)
    y = dot(
        jnp.concatenate([high, low, high], axis=1), jnp.concatenate([m_high, m_high, m_low], axis=0)
    )
    high, low = split(y)
    high, low = columns(high), columns(low)
    m_high, m_low = tabs[left, 0], tabs[left, 1]
    return dot(
        jnp.concatenate([m_high, m_high, m_low], axis=1), jnp.concatenate([high, low, high], axis=0)
    )


def times(a, b, px):
    ar, ai, br, bi = a[:px], a[px:], b[:px], b[px:]
    return jnp.concatenate([ar * br - ai * bi, ar * bi + ai * br], axis=0)


def conj_times(a, g, px):
    ar, ai, gr, gi = a[:px], a[px:], g[:px], g[px:]
    return jnp.concatenate([ar * gr + ai * gi, ar * gi - ai * gr], axis=0)


def kernel(
    n_tx, n_ty, n_sl, cap, all_positions,
    obj, probe, measured, list_r, list_c, owner, tabs,
    obj_out, probe_out,
    field, pat, staged, cut_c, put_c, patches, away, phis, grads, g_recv, lifted, placed,
    pieces, pg_mine, zone, deltas, wave, pg_sum,
    load_sem, pat_send, pat_recv, p_send, p_recv, g_send, g_rcv, pc_send, pc_recv, zn_send, zn_recv, dl_send, dl_recv,
):
    ix, iy, core = lax.axis_index("tx"), lax.axis_index("ty"), lax.axis_index("sl")
    layers, _, rows, cols = obj.shape
    positions, px, _ = measured.shape
    half = n_tx // n_sl
    slots = half * cap
    total = n_sl * layers
    other = 1 - core
    plane = n_ty * n_sl
    flat = iy * n_sl + core
    deep = 2 * px // plane
    peer = {"sl": other}

    def beside(d):
        i = lax.rem(flat + d, plane)
        return i, {"ty": i // n_sl, "sl": lax.rem(i, n_sl)}

    def along(d):
        i = lax.rem(ix + d, n_tx)
        return i, {"tx": i}

    def load(q):
        return [
            pltpu.make_async_copy(obj.at[q // 2, q % 2, :, lanes(j, px)], field.at[q, j], load_sem.at[q, j])
            for j in range(cols // px)
        ]

    for q in range(2 * layers):
        for copy in load(q):
            copy.start()

    barrier = pltpu.get_barrier_semaphore()
    for d in range(1, plane):
        pl.semaphore_signal(barrier, inc=1, device_id=beside(d)[1], device_id_type=MESH)
    for d in range(1, n_tx):
        pl.semaphore_signal(barrier, inc=1, device_id=along(d)[1], device_id_type=MESH)

    wave[...] = jnp.concatenate([probe[0], probe[1]], axis=0)

    def stage(o, carry):
        seen = jnp.int32(0)
        found = [jnp.int32(-1)] * cap
        for p in range(positions):
            here = owner[0, p] == o
            for k in range(cap):
                found[k] = jnp.where(here & (seen == k), jnp.int32(p), found[k])
            seen = seen + jnp.where(here, 1, 0)
        for k in range(cap):
            values = jnp.full((px, px), -1.0, F32)
            for p in range(positions):
                values = jnp.where(found[k] == p, measured[p], values)
            staged[o, k] = values.astype(BF16)
        return carry

    lax.fori_loop(0, n_tx, stage, 0)

    def slot_corner(t, c):
        s, k = c * half + t // cap, t % cap
        return jnp.clip(list_r[k, 0, s], 0, rows - px), jnp.clip(list_c[k, 0, s], 0, cols - px)

    def hot(shape, axis, shift):
        long = lax.broadcasted_iota(jnp.int32, shape, axis)
        short = lax.broadcasted_iota(jnp.int32, shape, 1 - axis)
        return jnp.where(long - short == shift, 1.0, 0.0).astype(BF16)

    def column_block(col):
        return jnp.minimum(col // px, cols // px - 2)

    def build_cut(t):
        for at, c in ((t, core), (slots + t, other)):
            _, col = slot_corner(t, c)
            cut_c[at] = hot((2 * px, px), 0, col - column_block(col) * px)

    loop(slots, build_cut)
    for q in range(2 * layers):
        for copy in load(q):
            copy.wait()
    pl.semaphore_wait(barrier, plane - 1 + n_tx - 1)

    mine_sends = (ix // half) == core
    local_s = lax.rem(ix, half)

    def pattern_copy(o, s):
        return pltpu.make_async_remote_copy(
            src_ref=staged.at[o], dst_ref=pat.at[s], send_sem=pat_send.at[o], recv_sem=pat_recv.at[s],
            device_id={"tx": o}, device_id_type=MESH,
        )

    @pl.when(mine_sends)
    def _():
        for d in range(1, n_tx):
            pattern_copy(along(d)[0], local_s).start()
        pat[local_s] = staged[ix]

    def patch_copy(t):
        return pltpu.make_async_remote_copy(
            src_ref=away.at[:, :, lanes(t, px)],
            dst_ref=patches.at[pl.ds(core * layers, layers), :, lanes(t, px)],
            send_sem=p_send.at[t], recv_sem=p_recv.at[t], device_id=peer, device_id_type=MESH,
        )

    def grad_copy(it):
        return pltpu.make_async_remote_copy(
            src_ref=grads.at[pl.ds(other * layers, layers)], dst_ref=g_recv,
            send_sem=g_send.at[it], recv_sem=g_rcv.at[it], device_id=peer, device_id_type=MESH,
        )

    def piece_copy(it, d):
        i, where = beside(d)
        return pltpu.make_async_remote_copy(
            src_ref=pg_mine.at[it, pl.ds(pl.multiple_of(i * deep, deep), deep)], dst_ref=pieces.at[it, d],
            send_sem=pc_send.at[it, d], recv_sem=pc_recv.at[it, d], device_id=where, device_id_type=MESH,
        )

    def zone_copy(it, d):
        return pltpu.make_async_remote_copy(
            src_ref=zone.at[it, ix], dst_ref=zone.at[it, ix],
            send_sem=zn_send.at[it, d], recv_sem=zn_recv.at[it, d], device_id=along(d)[1], device_id_type=MESH,
        )

    own_rows = pl.ds(pl.multiple_of(flat * deep, deep), deep)

    def delta_copy(it, d):
        return pltpu.make_async_remote_copy(
            src_ref=deltas.at[it, own_rows], dst_ref=deltas.at[it, own_rows],
            send_sem=dl_send.at[it, d], recv_sem=dl_recv.at[it, d], device_id=beside(d)[1], device_id_type=MESH,
        )

    def plane_sum(it):
        add = pg_mine[it, own_rows].astype(F32)
        for d in range(1, plane):
            piece_copy(it, d).wait_recv()
            add = add + pieces[it, d].astype(F32)
        zone[it, ix] = add.astype(BF16)
        for d in range(1, n_tx):
            zone_copy(it, d).start()

    def whole_sum(it):
        for d in range(1, n_tx):
            zone_copy(it, d).wait_recv()
        add = zone[it, 0].astype(F32)
        for i in range(1, n_tx):
            add = add + zone[it, i].astype(F32)
        deltas[it, own_rows] = add.astype(BF16)
        for d in range(1, plane):
            delta_copy(it, d).start()

    def finish_probe(it):
        for d in range(1, plane):
            delta_copy(it, d).wait_recv()
        wave[...] -= (STEP_PROBE / all_positions) * deltas[it].astype(F32)

    def cut(it, t, c, at):
        row, col = slot_corner(t, c)
        first = column_block(col)
        held = jnp.concatenate(
            [
                jnp.concatenate(
                    [field[q, first + j, pl.ds(row, px), :].astype(BF16) for j in range(2)], axis=1
                )
                for q in range(2 * layers)
            ],
            axis=0,
        )
        return dot(held, cut_c[at]).astype(BF16)

    def build_put(t):
        _, col = slot_corner(t, core)
        put_c[lanes(t, px), :] = hot((px, cols), 1, col)
        _, col = slot_corner(t, other)
        put_c[lanes(slots + t, px), :] = hot((px, cols), 1, col)
        blank = jnp.zeros((rows - px, px), F32)
        for q in range(2 * layers):
            lifted[t, q, pl.ds(0, rows - px), :] = blank
            lifted[t, q, pl.ds(rows, rows - px), :] = blank

    chunk = max(d for d in range(1, 7) if slots % d == 0)
    fine_chunk = 2 if chunk % 2 == 0 else 1
    width = fine_chunk * px

    for it in range(ITERS):
        def cut_away(t):
            if it > 0:
                patch_copy(t).wait_send()
            done = cut(it, t, other, slots + t)
            for q in range(2 * layers):
                away[q // 2, q % 2 * px : (q % 2 + 1) * px, lanes(t, px)] = done[q * px : (q + 1) * px]
            patch_copy(t).start()

        def cut_own(t):
            done = cut(it, t, core, t)
            for q in range(2 * layers):
                patches[core * layers + q // 2, q % 2 * px : (q % 2 + 1) * px, lanes(t, px)] = (
                    done[q * px : (q + 1) * px]
                )

        loop(slots, cut_away)
        loop(slots, cut_own)
        if it == 0:
            loop(slots, build_put)
        if it > 0:
            finish_probe(it - 1)
        loop(slots, lambda t: patch_copy(t).wait_recv())

        def wait_patterns():
            def arrive(i, carry):
                @pl.when(core * half + i != ix)
                def _():
                    pattern_copy(ix, i).wait_recv()

                return carry

            lax.fori_loop(0, half, arrive, 0)

        if it == 0:
            wait_patterns()

        pg_sum[...] = jnp.zeros_like(pg_sum)

        def run(k):
            first = k * chunk
            spans = [lanes(first // fine_chunk + i, width) for i in range(chunk // fine_chunk)]
            w = jnp.concatenate([wave[...]] * fine_chunk, axis=1)
            psi = [times(w, patches[0, :, span].astype(F32), px) for span in spans]
            for l in range(1, total):
                for i, span in enumerate(spans):
                    phi = both_sides(psi[i], tabs, 0, 1, px)
                    phis[l - 1, :, span] = phi
                    psi[i] = times(phi, patches[l, :, span].astype(F32), px)
            g = []
            for i in range(len(spans)):
                far = both_sides(psi[i], tabs, 2, 3, px)
                target = []
                for s in range(fine_chunk):
                    t = first + i * fine_chunk + s
                    target.append(pat[t // cap, t % cap].astype(F32))
                target = jnp.concatenate(target, axis=1)
                fr, fi = far[:px], far[px:]
                miss = jnp.where(target >= 0.0, 2.0 * (fr * fr + fi * fi - target), 0.0)
                g.append(jnp.concatenate([miss * fr, miss * fi], axis=0))
            g = [both_sides(one, tabs, 3, 2, px, fine=False) for one in g]
            for l in range(total - 1, -1, -1):
                for i, span in enumerate(spans):
                    before = phis[l - 1, :, span] if l else w
                    grads[l, :, span] = conj_times(before, g[i], px).astype(BF16)
                    g[i] = conj_times(patches[l, :, span].astype(F32), g[i], px)
                    if l:
                        g[i] = both_sides(g[i], tabs, 1, 0, px, fine=False)
            for one in g:
                for s in range(fine_chunk):
                    pg_sum[...] += one[:, s * px : (s + 1) * px]

        if it > 0:
            grad_copy(it - 1).wait_send()
        loop(slots // chunk, run)

        pg_mine[it] = pg_sum[...].astype(BF16)
        for d in range(1, plane):
            piece_copy(it, d).start()
        grad_copy(it).start()

        def place(source, first, base, c, last):
            def lift(t):
                for q in range(2 * layers):
                    lifted[t, q, pl.ds(rows - px, px), :] = (
                        source[first + q // 2, q % 2 * px : (q % 2 + 1) * px, lanes(t, px)].astype(F32)
                    )

            def spread(t):
                row, _ = slot_corner(t, c)
                for q in range(2 * layers):
                    placed[q, :, lanes(base + t, px)] = lifted[t, q, pl.ds(rows - px - row, rows), :].astype(BF16)

            loop(slots, lift)
            loop(slots, spread)
            span = pl.ds(base * px, slots * px)
            for q in range(2 * layers):
                add = STEP_OBJECT * dot(placed[q, :, span], put_c[span, :])
                for j in range(cols // px):
                    now = field[q, j] - add[:, j * px : (j + 1) * px]
                    if last:
                        obj_out[q // 2, q % 2, :, lanes(j, px)] = now
                    else:
                        field[q, j] = now

        place(grads, core * layers, 0, core, False)
        plane_sum(it)
        grad_copy(it).wait_recv()
        place(g_recv, 0, slots, other, it == ITERS - 1)
        whole_sum(it)

    finish_probe(ITERS - 1)
    probe_out[0] = wave[:px]
    probe_out[1] = wave[px:]

    @pl.when(mine_sends)
    def _():
        for d in range(1, n_tx):
            pattern_copy(along(d)[0], local_s).wait_send()

    loop(slots, lambda t: patch_copy(t).wait_send())
    grad_copy(ITERS - 1).wait_send()
    for it in range(ITERS):
        for d in range(1, plane):
            piece_copy(it, d).wait_send()
            delta_copy(it, d).wait_send()
        for d in range(1, n_tx):
            zone_copy(it, d).wait_send()


def body(object_field, probe_wave, measured, owner_row, list_rows, list_cols):
    layers, _, rows, cols = object_field.shape
    positions, px, _ = measured.shape
    n_tx, n_ty, n_sl = lax.axis_size("tx"), lax.axis_size("ty"), lax.axis_size("sl")
    cap = list_rows.shape[-1]
    half = n_tx // n_sl
    slots = half * cap
    total = n_sl * layers
    plane = n_ty * n_sl
    deep = 2 * px // plane
    tabs = jnp.asarray(real_tables(px))
    tables = [jnp.transpose(one, (0, 3, 1, 2)).reshape(cap, 1, n_tx) for one in (list_rows, list_cols)]
    vmem = pl.BlockSpec(memory_space=pltpu.VMEM)
    smem = pl.BlockSpec(memory_space=pltpu.SMEM)
    dma = pltpu.SemaphoreType.DMA
    return pl.pallas_call(
        functools.partial(kernel, n_tx, n_ty, n_sl, cap, positions * n_tx * n_ty),
        out_shape=(
            pltpu.VMEM(object_field.shape, F32),
            pltpu.VMEM(probe_wave.shape, F32),
        ),
        in_specs=[pl.BlockSpec(memory_space=pl.ANY), vmem, vmem, smem, smem, smem, vmem],
        out_specs=(vmem, vmem),
        scratch_shapes=[
            pltpu.VMEM((2 * layers, cols // px, rows, px), F32),
            pltpu.VMEM((half, cap, px, px), BF16),
            pltpu.VMEM((n_tx, cap, px, px), BF16),
            pltpu.VMEM((2 * slots, 2 * px, px), BF16),
            pltpu.VMEM((2 * slots * px, cols), BF16),
            pltpu.VMEM((total, 2 * px, slots * px), BF16),
            pltpu.VMEM((layers, 2 * px, slots * px), BF16),
            pltpu.VMEM((total - 1, 2 * px, slots * px), F32),
            pltpu.VMEM((total, 2 * px, slots * px), BF16),
            pltpu.VMEM((layers, 2 * px, slots * px), BF16),
            pltpu.VMEM((slots, 2 * layers, 2 * rows - px, px), F32),
            pltpu.VMEM((2 * layers, rows, 2 * slots * px), BF16),
            pltpu.VMEM((ITERS, plane, deep, px), BF16),
            pltpu.VMEM((ITERS, 2 * px, px), BF16),
            pltpu.VMEM((ITERS, n_tx, deep, px), BF16),
            pltpu.VMEM((ITERS, 2 * px, px), BF16),
            pltpu.VMEM((2 * px, px), F32),
            pltpu.VMEM((2 * px, px), F32),
            dma((2 * layers, cols // px)),
            dma((n_tx,)),
            dma((half,)),
            dma((slots,)),
            dma((slots,)),
            dma((ITERS,)),
            dma((ITERS,)),
            dma((ITERS, plane)),
            dma((ITERS, plane)),
            dma((ITERS, n_tx)),
            dma((ITERS, n_tx)),
            dma((ITERS, plane)),
            dma((ITERS, plane)),
        ],
        compiler_params=pltpu.CompilerParams(
            collective_id=0, has_side_effects=True, vmem_limit_bytes=58 * 2**20
        ),
    )(object_field, probe_wave, measured, *tables, owner_row.reshape(1, -1), tabs)


def solution(mesh):
    in_specs = (
        P(("groups", "sl"), None, "tx", "ty"),
        P("groups", None, None),
        P(("groups", "tx", "ty"), None, None),
        P(("groups", "tx", "ty"), None),
        P(("groups", "tx"), "ty", None, None),
        P(("groups", "tx"), "ty", None, None),
    )
    out_specs = (P(("groups", "sl"), None, "tx", "ty"), P("groups", None, None))
    return jax.shard_map(body, mesh=mesh, in_specs=in_specs, out_specs=out_specs, check_vma=False)
```

```python
import functools
import math

import jax
import jax.numpy as jnp
import numpy as np
from jax import lax
from jax.experimental import pallas as pl
from jax.experimental.pallas import tpu as pltpu
from jax.sharding import PartitionSpec as P

ITERS = 2
PHASE = 0.25
STEP_OBJECT = 0.01
STEP_PROBE = 0.6
KERN_SCALE = 1.6465
F32 = jnp.float32
BF16 = jnp.bfloat16
MESH = pl.DeviceIdType.MESH


def real_tables(pixels):
    index = np.arange(pixels)
    four = np.exp(-2j * math.pi * ((index[:, None] * index[None, :]) % pixels) / pixels) / math.sqrt(pixels)
    freq = np.where(index < pixels // 2, index, index - pixels).astype(np.float64)
    kern = (np.conj(four) * np.exp(-1j * PHASE * freq * freq / pixels)[None, :]) @ four
    found = []
    for matrix in (KERN_SCALE * kern, math.sqrt(pixels) * four):
        right = np.block([[matrix.real, matrix.imag], [-matrix.imag, matrix.real]])
        found += [right, right.T]
    whole = np.stack(found).astype(np.float32)
    high = whole.astype(jnp.bfloat16)
    low = (whole - high.astype(np.float32)).astype(jnp.bfloat16)
    return np.stack([high, low], axis=1)


def split(x):
    high = x.astype(BF16)
    return high, (x - high.astype(F32)).astype(BF16)


def dot(a, b):
    return jnp.dot(a, b, preferred_element_type=F32)


def loop(count, step):
    if count <= 8:
        for i in range(count):
            step(i)
    else:
        lax.fori_loop(0, count, lambda i, carry: (step(i), carry)[1], 0)


def lanes(i, width):
    return pl.ds(i * width if isinstance(i, int) else pl.multiple_of(i * width, width), width)


def both_sides(x, tabs, right, left, px, passes):
    count = x.shape[1] // px
    scale = 1.0 / px if right >= 2 else KERN_SCALE**-2

    def rows(v):
        return jnp.concatenate(
            [
                jnp.concatenate([v[:px, s * px : (s + 1) * px], v[px:, s * px : (s + 1) * px]], axis=1)
                for s in range(count)
            ],
            axis=0,
        )

    def columns(v):
        return jnp.concatenate(
            [
                jnp.concatenate([v[s * px : (s + 1) * px, :px], v[s * px : (s + 1) * px, px:]], axis=0)
                for s in range(count)
            ],
            axis=1,
        )

    m_high, m_low = tabs[right, 0], tabs[right, 1]
    n_high, n_low = tabs[left, 0], tabs[left, 1]
    if passes == 1:
        y = dot(rows(x.astype(BF16)), m_high)
        return scale * dot(n_high, columns(y.astype(BF16)))
    if passes == 2:
        v = rows(x.astype(BF16))
        y = dot(jnp.concatenate([v, v], axis=1), jnp.concatenate([m_high, m_low], axis=0))
        v = columns(y.astype(BF16))
        return scale * dot(jnp.concatenate([n_high, n_low], axis=1), jnp.concatenate([v, v], axis=0))
    high, low = split(x)
    high, low = rows(high), rows(low)
    y = dot(
        jnp.concatenate([high, low, high], axis=1), jnp.concatenate([m_high, m_high, m_low], axis=0)
    )
    high, low = split(y)
    high, low = columns(high), columns(low)
    return scale * dot(
        jnp.concatenate([n_high, n_high, n_low], axis=1), jnp.concatenate([high, low, high], axis=0)
    )


def times(a, b, px):
    ar, ai, br, bi = a[:px], a[px:], b[:px], b[px:]
    return jnp.concatenate([ar * br - ai * bi, ar * bi + ai * br], axis=0)


def conj_times(a, g, px):
    ar, ai, gr, gi = a[:px], a[px:], g[:px], g[px:]
    return jnp.concatenate([ar * gr + ai * gi, ar * gi - ai * gr], axis=0)


def kernel(
    n_tx, n_ty, n_sl, cap, all_positions,
    obj, probe, measured_at, list_r, list_c, owner, tabs_at,
    obj_out, probe_out,
    field, measured, tabs, pat, staged, cut_c, put_c, patches, away, phis, grads, g_recv, lifted, placed,
    pieces, pg_mine, zone, deltas, wave, pg_sum,
    load_sem, in_sem, pat_send, pat_recv, p_send, p_recv, g_send, g_rcv, pc_send, pc_recv, zn_send, zn_recv, dl_send, dl_recv,
):
    ix, iy, core = lax.axis_index("tx"), lax.axis_index("ty"), lax.axis_index("sl")
    layers, _, rows, cols = obj.shape
    positions, px, _ = measured.shape
    half = n_tx // n_sl
    slots = half * cap
    total = n_sl * layers
    other = 1 - core
    plane = n_ty * n_sl
    flat = iy * n_sl + core
    deep = 2 * px // plane
    peer = {"sl": other}

    def beside(d):
        i = lax.rem(flat + d, plane)
        return i, {"ty": i // n_sl, "sl": lax.rem(i, n_sl)}

    def along(d):
        i = lax.rem(ix + d, n_tx)
        return i, {"tx": i}

    def load(q):
        return [
            pltpu.make_async_copy(obj.at[q // 2, q % 2, :, lanes(j, px)], field.at[q, j], load_sem.at[q, j])
            for j in range(cols // px)
        ]

    for q in range(2 * layers):
        for copy in load(q):
            copy.start()

    measured_load = pltpu.make_async_copy(measured_at, measured, in_sem.at[0])
    tabs_load = pltpu.make_async_copy(tabs_at, tabs, in_sem.at[1])
    measured_load.start()
    tabs_load.start()

    barrier = pltpu.get_barrier_semaphore()
    for d in range(1, plane):
        pl.semaphore_signal(barrier, inc=1, device_id=beside(d)[1], device_id_type=MESH)
    for d in range(1, n_tx):
        pl.semaphore_signal(barrier, inc=1, device_id=along(d)[1], device_id_type=MESH)

    wave[...] = jnp.concatenate([probe[0], probe[1]], axis=0)

    def stage(o, carry):
        seen = jnp.int32(0)
        found = [jnp.int32(-1)] * cap
        for p in range(positions):
            here = owner[0, p] == o
            for k in range(cap):
                found[k] = jnp.where(here & (seen == k), jnp.int32(p), found[k])
            seen = seen + jnp.where(here, 1, 0)
        for k in range(cap):
            values = jnp.full((px, px), -1.0, F32)
            for p in range(positions):
                values = jnp.where(found[k] == p, measured[p], values)
            staged[o, k] = values.astype(BF16)
        return carry


    def slot_corner(t, c):
        s, k = c * half + t // cap, t % cap
        return jnp.clip(list_r[k, 0, s], 0, rows - px), jnp.clip(list_c[k, 0, s], 0, cols - px)

    def hot(shape, axis, shift):
        long = lax.broadcasted_iota(jnp.int32, shape, axis)
        short = lax.broadcasted_iota(jnp.int32, shape, 1 - axis)
        return jnp.where(long - short == shift, 1.0, 0.0).astype(BF16)

    def column_block(col):
        return jnp.minimum(col // px, cols // px - 2)

    def build_cut(t):
        for at, c in ((t, core), (slots + t, other)):
            _, col = slot_corner(t, c)
            cut_c[at] = hot((2 * px, px), 0, col - column_block(col) * px)

    loop(slots, build_cut)
    measured_load.wait()
    lax.fori_loop(0, n_tx, stage, 0)
    for q in range(2 * layers):
        for copy in load(q):
            copy.wait()
    pl.semaphore_wait(barrier, plane - 1 + n_tx - 1)

    mine_sends = (ix // half) == core
    local_s = lax.rem(ix, half)

    def pattern_copy(o, s):
        return pltpu.make_async_remote_copy(
            src_ref=staged.at[o], dst_ref=pat.at[s], send_sem=pat_send.at[o], recv_sem=pat_recv.at[s],
            device_id={"tx": o}, device_id_type=MESH,
        )

    @pl.when(mine_sends)
    def _():
        for d in range(1, n_tx):
            pattern_copy(along(d)[0], local_s).start()
        pat[local_s] = staged[ix]

    def patch_copy(t):
        return pltpu.make_async_remote_copy(
            src_ref=away.at[:, :, lanes(t, px)],
            dst_ref=patches.at[pl.ds(core * layers, layers), :, lanes(t, px)],
            send_sem=p_send.at[t], recv_sem=p_recv.at[t], device_id=peer, device_id_type=MESH,
        )

    def grad_copy(it):
        return pltpu.make_async_remote_copy(
            src_ref=grads.at[pl.ds(other * layers, layers)], dst_ref=g_recv,
            send_sem=g_send.at[it], recv_sem=g_rcv.at[it], device_id=peer, device_id_type=MESH,
        )

    def piece_copy(it, d):
        i, where = beside(d)
        return pltpu.make_async_remote_copy(
            src_ref=pg_mine.at[it, pl.ds(pl.multiple_of(i * deep, deep), deep)], dst_ref=pieces.at[it, d],
            send_sem=pc_send.at[it, d], recv_sem=pc_recv.at[it, d], device_id=where, device_id_type=MESH,
        )

    def zone_copy(it, d):
        return pltpu.make_async_remote_copy(
            src_ref=zone.at[it, ix], dst_ref=zone.at[it, ix],
            send_sem=zn_send.at[it, d], recv_sem=zn_recv.at[it, d], device_id=along(d)[1], device_id_type=MESH,
        )

    own_rows = pl.ds(pl.multiple_of(flat * deep, deep), deep)

    def delta_copy(it, d):
        return pltpu.make_async_remote_copy(
            src_ref=deltas.at[it, own_rows], dst_ref=deltas.at[it, own_rows],
            send_sem=dl_send.at[it, d], recv_sem=dl_recv.at[it, d], device_id=beside(d)[1], device_id_type=MESH,
        )

    def plane_sum(it):
        add = pg_mine[it, own_rows].astype(F32)
        for d in range(1, plane):
            piece_copy(it, d).wait_recv()
            add = add + pieces[it, d].astype(F32)
        zone[it, ix] = add.astype(BF16)
        for d in range(1, n_tx):
            zone_copy(it, d).start()

    def whole_sum(it):
        for d in range(1, n_tx):
            zone_copy(it, d).wait_recv()
        add = zone[it, 0].astype(F32)
        for i in range(1, n_tx):
            add = add + zone[it, i].astype(F32)
        deltas[it, own_rows] = add.astype(BF16)
        for d in range(1, plane):
            delta_copy(it, d).start()

    def finish_probe(it):
        for d in range(1, plane):
            delta_copy(it, d).wait_recv()
        wave[...] -= (STEP_PROBE / all_positions) * deltas[it].astype(F32)

    def cut(it, t, c, at):
        row, col = slot_corner(t, c)
        first = column_block(col)
        held = jnp.concatenate(
            [
                jnp.concatenate(
                    [field[q, first + j, pl.ds(row, px), :].astype(BF16) for j in range(2)], axis=1
                )
                for q in range(2 * layers)
            ],
            axis=0,
        )
        return dot(held, cut_c[at]).astype(BF16)

    def build_put(t):
        _, col = slot_corner(t, core)
        put_c[lanes(t, px), :] = hot((px, cols), 1, col)
        _, col = slot_corner(t, other)
        put_c[lanes(slots + t, px), :] = hot((px, cols), 1, col)
        blank = jnp.zeros((rows - px, px), F32)
        for q in range(2 * layers):
            lifted[t, q, pl.ds(0, rows - px), :] = blank
            lifted[t, q, pl.ds(rows, rows - px), :] = blank

    chunk = max(d for d in range(1, 7) if slots % d == 0)
    fine_chunk = 2 if chunk % 2 == 0 else 1
    width = fine_chunk * px
    runs = slots // chunk

    for it in range(ITERS):
        forth, back = (2, 1) if it == ITERS - 1 else (3, 2)

        def cut_away(t):
            if it > 0:
                patch_copy(t).wait_send()
            done = cut(it, t, other, slots + t)
            for q in range(2 * layers):
                away[q // 2, q % 2 * px : (q % 2 + 1) * px, lanes(t, px)] = done[q * px : (q + 1) * px]
            patch_copy(t).start()

        def cut_own(t):
            done = cut(it, t, core, t)
            for q in range(2 * layers):
                patches[core * layers + q // 2, q % 2 * px : (q % 2 + 1) * px, lanes(t, px)] = (
                    done[q * px : (q + 1) * px]
                )

        loop(slots, cut_away)
        loop(slots, cut_own)
        if it == 0:
            loop(slots, build_put)
        if it > 0:
            whole_sum(it - 1)
            finish_probe(it - 1)
        loop(slots, lambda t: patch_copy(t).wait_recv())

        def wait_patterns():
            def arrive(i, carry):
                @pl.when(core * half + i != ix)
                def _():
                    pattern_copy(ix, i).wait_recv()

                return carry

            lax.fori_loop(0, half, arrive, 0)

        if it == 0:
            tabs_load.wait()
            if runs > 8:
                wait_patterns()

        pg_sum[...] = jnp.zeros_like(pg_sum)

        def run(k):
            first = k * chunk
            spans = [lanes(first // fine_chunk + i, width) for i in range(chunk // fine_chunk)]
            w = jnp.concatenate([wave[...]] * fine_chunk, axis=1)
            psi = [times(w, patches[0, :, span].astype(F32), px) for span in spans]
            for l in range(1, total):
                for i, span in enumerate(spans):
                    phi = both_sides(psi[i], tabs, 0, 1, px, forth)
                    phis[l - 1, :, span] = phi
                    psi[i] = times(phi, patches[l, :, span].astype(F32), px)
            if it == 0 and runs <= 8 and k == 0:
                wait_patterns()
            g = []
            for i in range(len(spans)):
                far = both_sides(psi[i], tabs, 2, 3, px, forth)
                target = []
                for s in range(fine_chunk):
                    t = first + i * fine_chunk + s
                    target.append(pat[t // cap, t % cap].astype(F32))
                target = jnp.concatenate(target, axis=1)
                fr, fi = far[:px], far[px:]
                miss = jnp.where(target >= 0.0, 2.0 * (fr * fr + fi * fi - target), 0.0)
                g.append(jnp.concatenate([miss * fr, miss * fi], axis=0))
            g = [both_sides(one, tabs, 3, 2, px, back) for one in g]
            for l in range(total - 1, -1, -1):
                for i, span in enumerate(spans):
                    before = phis[l - 1, :, span] if l else w
                    grads[l, :, span] = conj_times(before, g[i], px).astype(BF16)
                    g[i] = conj_times(patches[l, :, span].astype(F32), g[i], px)
                    if l:
                        g[i] = both_sides(g[i], tabs, 1, 0, px, back)
            for one in g:
                for s in range(fine_chunk):
                    pg_sum[...] += one[:, s * px : (s + 1) * px]

        if it > 0:
            grad_copy(it - 1).wait_send()
        loop(runs, run)

        pg_mine[it] = pg_sum[...].astype(BF16)
        for d in range(1, plane):
            piece_copy(it, d).start()
        grad_copy(it).start()

        def place(source, first, base, c, last):
            def lift(t):
                for q in range(2 * layers):
                    lifted[t, q, pl.ds(rows - px, px), :] = (
                        source[first + q // 2, q % 2 * px : (q % 2 + 1) * px, lanes(t, px)].astype(F32)
                    )

            def spread(t):
                row, _ = slot_corner(t, c)
                for q in range(2 * layers):
                    placed[q, :, lanes(base + t, px)] = lifted[t, q, pl.ds(rows - px - row, rows), :].astype(BF16)

            loop(slots, lift)
            loop(slots, spread)
            span = pl.ds(base * px, slots * px)
            for q in range(2 * layers):
                add = STEP_OBJECT * dot(placed[q, :, span], put_c[span, :])
                for j in range(cols // px):
                    now = field[q, j] - add[:, j * px : (j + 1) * px]
                    if last:
                        obj_out[q // 2, q % 2, :, lanes(j, px)] = now
                    else:
                        field[q, j] = now

        place(grads, core * layers, 0, core, False)
        plane_sum(it)
        grad_copy(it).wait_recv()
        place(g_recv, 0, slots, other, it == ITERS - 1)

    whole_sum(ITERS - 1)
    finish_probe(ITERS - 1)
    probe_out[0] = wave[:px]
    probe_out[1] = wave[px:]

    @pl.when(mine_sends)
    def _():
        for d in range(1, n_tx):
            pattern_copy(along(d)[0], local_s).wait_send()

    loop(slots, lambda t: patch_copy(t).wait_send())
    grad_copy(ITERS - 1).wait_send()
    for it in range(ITERS):
        for d in range(1, plane):
            piece_copy(it, d).wait_send()
            delta_copy(it, d).wait_send()
        for d in range(1, n_tx):
            zone_copy(it, d).wait_send()


def body(object_field, probe_wave, measured, owner_row, list_rows, list_cols):
    layers, _, rows, cols = object_field.shape
    positions, px, _ = measured.shape
    n_tx, n_ty, n_sl = lax.axis_size("tx"), lax.axis_size("ty"), lax.axis_size("sl")
    cap = list_rows.shape[-1]
    half = n_tx // n_sl
    slots = half * cap
    total = n_sl * layers
    plane = n_ty * n_sl
    deep = 2 * px // plane
    tabs = jnp.asarray(real_tables(px))
    tables = [jnp.transpose(one, (0, 3, 1, 2)).reshape(cap, 1, n_tx) for one in (list_rows, list_cols)]
    vmem = pl.BlockSpec(memory_space=pltpu.VMEM)
    anywhere = pl.BlockSpec(memory_space=pl.ANY)
    smem = pl.BlockSpec(memory_space=pltpu.SMEM)
    dma = pltpu.SemaphoreType.DMA
    return pl.pallas_call(
        functools.partial(kernel, n_tx, n_ty, n_sl, cap, positions * n_tx * n_ty),
        out_shape=(
            pltpu.VMEM(object_field.shape, F32),
            pltpu.VMEM(probe_wave.shape, F32),
        ),
        in_specs=[anywhere, vmem, anywhere, smem, smem, smem, anywhere],
        out_specs=(vmem, vmem),
        scratch_shapes=[
            pltpu.VMEM((2 * layers, cols // px, rows, px), F32),
            pltpu.VMEM(measured.shape, F32),
            pltpu.VMEM(tabs.shape, BF16),
            pltpu.VMEM((half, cap, px, px), BF16),
            pltpu.VMEM((n_tx, cap, px, px), BF16),
            pltpu.VMEM((2 * slots, 2 * px, px), BF16),
            pltpu.VMEM((2 * slots * px, cols), BF16),
            pltpu.VMEM((total, 2 * px, slots * px), BF16),
            pltpu.VMEM((layers, 2 * px, slots * px), BF16),
            pltpu.VMEM((total - 1, 2 * px, slots * px), F32),
            pltpu.VMEM((total, 2 * px, slots * px), BF16),
            pltpu.VMEM((layers, 2 * px, slots * px), BF16),
            pltpu.VMEM((slots, 2 * layers, 2 * rows - px, px), F32),
            pltpu.VMEM((2 * layers, rows, 2 * slots * px), BF16),
            pltpu.VMEM((ITERS, plane, deep, px), BF16),
            pltpu.VMEM((ITERS, 2 * px, px), BF16),
            pltpu.VMEM((ITERS, n_tx, deep, px), BF16),
            pltpu.VMEM((ITERS, 2 * px, px), BF16),
            pltpu.VMEM((2 * px, px), F32),
            pltpu.VMEM((2 * px, px), F32),
            dma((2 * layers, cols // px)),
            dma((2,)),
            dma((n_tx,)),
            dma((half,)),
            dma((slots,)),
            dma((slots,)),
            dma((ITERS,)),
            dma((ITERS,)),
            dma((ITERS, plane)),
            dma((ITERS, plane)),
            dma((ITERS, n_tx)),
            dma((ITERS, n_tx)),
            dma((ITERS, plane)),
            dma((ITERS, plane)),
        ],
        compiler_params=pltpu.CompilerParams(
            collective_id=0, has_side_effects=True, vmem_limit_bytes=58 * 2**20
        ),
    )(object_field, probe_wave, measured, *tables, owner_row.reshape(1, -1), tabs)


def solution(mesh):
    in_specs = (
        P(("groups", "sl"), None, "tx", "ty"),
        P("groups", None, None),
        P(("groups", "tx", "ty"), None, None),
        P(("groups", "tx", "ty"), None),
        P(("groups", "tx"), "ty", None, None),
        P(("groups", "tx"), "ty", None, None),
    )
    out_specs = (P(("groups", "sl"), None, "tx", "ty"), P("groups", None, None))
    return jax.shard_map(body, mesh=mesh, in_specs=in_specs, out_specs=out_specs, check_vma=False)
```

```python
import functools
import math

import jax
import jax.numpy as jnp
import numpy as np
from jax import lax
from jax.experimental import pallas as pl
from jax.experimental.pallas import tpu as pltpu
from jax.sharding import PartitionSpec as P

ITERS = 2
PHASE = 0.25
STEP_OBJECT = 0.01
STEP_PROBE = 0.6
KERN_SCALE = 1.6465
F32 = jnp.float32
BF16 = jnp.bfloat16
MESH = pl.DeviceIdType.MESH


def real_tables(pixels):
    index = np.arange(pixels)
    four = np.exp(-2j * math.pi * ((index[:, None] * index[None, :]) % pixels) / pixels) / math.sqrt(pixels)
    freq = np.where(index < pixels // 2, index, index - pixels).astype(np.float64)
    kern = (np.conj(four) * np.exp(-1j * PHASE * freq * freq / pixels)[None, :]) @ four
    found = []
    for matrix in (KERN_SCALE * kern, math.sqrt(pixels) * four):
        right = np.block([[matrix.real, matrix.imag], [-matrix.imag, matrix.real]])
        found += [right, right.T]
    whole = np.stack(found).astype(np.float32)
    high = whole.astype(jnp.bfloat16)
    low = (whole - high.astype(np.float32)).astype(jnp.bfloat16)
    return np.stack([high, low], axis=1)


def split(x):
    high = x.astype(BF16)
    return high, (x - high.astype(F32)).astype(BF16)


def dot(a, b):
    return jnp.dot(a, b, preferred_element_type=F32)


def loop(count, step):
    if count <= 8:
        for i in range(count):
            step(i)
    else:
        lax.fori_loop(0, count, lambda i, carry: (step(i), carry)[1], 0)


def lanes(i, width):
    return pl.ds(i * width if isinstance(i, int) else pl.multiple_of(i * width, width), width)


def both_sides(x, tabs, right, left, px, passes):
    count = x.shape[1] // px
    scale = 1.0 / px if right >= 2 else KERN_SCALE**-2

    def rows(v):
        return jnp.concatenate(
            [
                jnp.concatenate([v[:px, s * px : (s + 1) * px], v[px:, s * px : (s + 1) * px]], axis=1)
                for s in range(count)
            ],
            axis=0,
        )

    def columns(v):
        return jnp.concatenate(
            [
                jnp.concatenate([v[s * px : (s + 1) * px, :px], v[s * px : (s + 1) * px, px:]], axis=0)
                for s in range(count)
            ],
            axis=1,
        )

    m_high, m_low = tabs[right, 0], tabs[right, 1]
    n_high, n_low = tabs[left, 0], tabs[left, 1]
    if passes == 1:
        y = dot(rows(x.astype(BF16)), m_high)
        return scale * dot(n_high, columns(y.astype(BF16)))
    if passes == 2:
        v = rows(x.astype(BF16))
        y = dot(jnp.concatenate([v, v], axis=1), jnp.concatenate([m_high, m_low], axis=0))
        v = columns(y.astype(BF16))
        return scale * dot(jnp.concatenate([n_high, n_low], axis=1), jnp.concatenate([v, v], axis=0))
    high, low = split(x)
    high, low = rows(high), rows(low)
    y = dot(
        jnp.concatenate([high, low, high], axis=1), jnp.concatenate([m_high, m_high, m_low], axis=0)
    )
    high, low = split(y)
    high, low = columns(high), columns(low)
    return scale * dot(
        jnp.concatenate([n_high, n_high, n_low], axis=1), jnp.concatenate([high, low, high], axis=0)
    )


def times(a, b, px):
    ar, ai, br, bi = a[:px], a[px:], b[:px], b[px:]
    return jnp.concatenate([ar * br - ai * bi, ar * bi + ai * br], axis=0)


def conj_times(a, g, px):
    ar, ai, gr, gi = a[:px], a[px:], g[:px], g[px:]
    return jnp.concatenate([ar * gr + ai * gi, ar * gi - ai * gr], axis=0)


def kernel(
    n_tx, n_ty, n_sl, cap, all_positions,
    obj, probe, measured_at, list_r, list_c, owner, tabs_at,
    obj_out, probe_out,
    field, measured, tabs, pat, staged, cut_c, put_c, patches, away, phis, grads, g_recv, lifted, placed,
    pieces, pg_mine, zone, deltas, wave, pg_sum,
    load_sem, in_sem, pat_send, pat_recv, p_send, p_recv, g_send, g_rcv, pc_send, pc_recv, zn_send, zn_recv, dl_send, dl_recv,
):
    ix, iy, core = lax.axis_index("tx"), lax.axis_index("ty"), lax.axis_index("sl")
    layers, _, rows, cols = obj.shape
    positions, px, _ = measured.shape
    half = n_tx // n_sl
    slots = half * cap
    total = n_sl * layers
    other = 1 - core
    plane = n_ty * n_sl
    flat = iy * n_sl + core
    deep = 2 * px // n_sl
    peer = {"sl": other}

    def beside(d):
        i = lax.rem(flat + d, plane)
        return i, {"ty": i // n_sl, "sl": lax.rem(i, n_sl)}

    def along(d):
        i = lax.rem(ix + d, n_tx)
        return i, {"tx": i}

    barrier = pltpu.get_barrier_semaphore()
    for d in range(1, plane):
        pl.semaphore_signal(barrier, inc=1, device_id=beside(d)[1], device_id_type=MESH)
    for d in range(1, n_tx):
        pl.semaphore_signal(barrier, inc=1, device_id=along(d)[1], device_id_type=MESH)

    def load(q):
        return [
            pltpu.make_async_copy(obj.at[q // 2, q % 2, :, lanes(j, px)], field.at[q, j], load_sem.at[q, j])
            for j in range(cols // px)
        ]

    for q in range(2 * layers):
        for copy in load(q):
            copy.start()

    measured_load = pltpu.make_async_copy(measured_at, measured, in_sem.at[0])
    tabs_load = pltpu.make_async_copy(tabs_at, tabs, in_sem.at[1])
    measured_load.start()
    tabs_load.start()
    probe_loads = [
        pltpu.make_async_copy(probe.at[part], wave.at[pl.ds(part * px, px)], in_sem.at[2 + part]) for part in range(2)
    ]
    for copy in probe_loads:
        copy.start()


    def stage(o, carry):
        seen = jnp.int32(0)
        found = [jnp.int32(-1)] * cap
        for p in range(positions):
            here = owner[0, p] == o
            for k in range(cap):
                found[k] = jnp.where(here & (seen == k), jnp.int32(p), found[k])
            seen = seen + jnp.where(here, 1, 0)
        for k in range(cap):
            values = jnp.full((px, px), -1.0, F32)
            for p in range(positions):
                values = jnp.where(found[k] == p, measured[p], values)
            staged[o, k] = values.astype(BF16)
        return carry


    def slot_corner(t, c):
        s, k = c * half + t // cap, t % cap
        return jnp.clip(list_r[k, 0, s], 0, rows - px), jnp.clip(list_c[k, 0, s], 0, cols - px)

    def hot(shape, axis, shift):
        long = lax.broadcasted_iota(jnp.int32, shape, axis)
        short = lax.broadcasted_iota(jnp.int32, shape, 1 - axis)
        return jnp.where(long - short == shift, 1.0, 0.0).astype(BF16)

    def column_block(col):
        return jnp.minimum(col // px, cols // px - 2)

    def build_cut(t):
        for at, c in ((t, core), (slots + t, other)):
            _, col = slot_corner(t, c)
            cut_c[at] = hot((2 * px, px), 0, col - column_block(col) * px)

    loop(slots, build_cut)
    measured_load.wait()
    lax.fori_loop(0, n_tx, stage, 0)
    for q in range(2 * layers):
        for copy in load(q):
            copy.wait()
    pl.semaphore_wait(barrier, plane - 1 + n_tx - 1)

    mine_sends = (ix // half) == core
    local_s = lax.rem(ix, half)

    def pattern_copy(o, s):
        return pltpu.make_async_remote_copy(
            src_ref=staged.at[o], dst_ref=pat.at[s], send_sem=pat_send.at[o], recv_sem=pat_recv.at[s],
            device_id={"tx": o}, device_id_type=MESH,
        )

    @pl.when(mine_sends)
    def _():
        for d in range(n_tx - 1, 0, -1):
            pattern_copy(along(d)[0], local_s).start()
        pat[local_s] = staged[ix]

    def patch_copy(t):
        return pltpu.make_async_remote_copy(
            src_ref=away.at[:, :, lanes(t, px)],
            dst_ref=patches.at[pl.ds(core * layers, layers), :, lanes(t, px)],
            send_sem=p_send.at[t], recv_sem=p_recv.at[t], device_id=peer, device_id_type=MESH,
        )

    def grad_copy(it):
        return pltpu.make_async_remote_copy(
            src_ref=grads.at[pl.ds(other * layers, layers)], dst_ref=g_recv,
            send_sem=g_send.at[it], recv_sem=g_rcv.at[it], device_id=peer, device_id_type=MESH,
        )

    own_rows = pl.ds(pl.multiple_of(core * deep, deep), deep)

    def piece_copy(it, d):
        i, where = beside(d)
        theirs = pl.ds(pl.multiple_of(lax.rem(i, n_sl) * deep, deep), deep)
        return pltpu.make_async_remote_copy(
            src_ref=pg_mine.at[it, theirs], dst_ref=pieces.at[it, flat],
            send_sem=pc_send.at[it, d], recv_sem=pc_recv.at[it, d], device_id=where, device_id_type=MESH,
        )

    def zone_copy(it, d):
        return pltpu.make_async_remote_copy(
            src_ref=zone.at[it, ix], dst_ref=zone.at[it, ix],
            send_sem=zn_send.at[it, d], recv_sem=zn_recv.at[it, d], device_id=along(d)[1], device_id_type=MESH,
        )

    def delta_copy(it):
        return pltpu.make_async_remote_copy(
            src_ref=deltas.at[it, own_rows], dst_ref=deltas.at[it, own_rows],
            send_sem=dl_send.at[it], recv_sem=dl_recv.at[it], device_id=peer, device_id_type=MESH,
        )

    def plane_sum(it):
        pieces[it, flat] = pg_mine[it, own_rows]
        for d in range(1, plane):
            piece_copy(it, d).wait_recv()
        add = pieces[it, 0].astype(F32)
        for i in range(1, plane):
            add = add + pieces[it, i].astype(F32)
        zone[it, ix] = add.astype(BF16)
        for d in range(1, n_tx):
            zone_copy(it, d).start()

    def whole_sum(it):
        for d in range(1, n_tx):
            zone_copy(it, d).wait_recv()
        add = zone[it, 0].astype(F32)
        for i in range(1, n_tx):
            add = add + zone[it, i].astype(F32)
        deltas[it, own_rows] = add
        delta_copy(it).start()

    def finish_probe(it):
        delta_copy(it).wait_recv()
        wave[...] -= (STEP_PROBE / all_positions) * deltas[it]

    def cut(it, t, c, at):
        row, col = slot_corner(t, c)
        first = column_block(col)
        held = jnp.concatenate(
            [
                jnp.concatenate(
                    [field[q, first + j, pl.ds(row, px), :].astype(BF16) for j in range(2)], axis=1
                )
                for q in range(2 * layers)
            ],
            axis=0,
        )
        return dot(held, cut_c[at]).astype(BF16)

    def build_put(t):
        _, col = slot_corner(t, core)
        put_c[lanes(t, px), :] = hot((px, cols), 1, col)
        _, col = slot_corner(t, other)
        put_c[lanes(slots + t, px), :] = hot((px, cols), 1, col)
        blank = jnp.zeros((rows - px, px), F32)
        for q in range(2 * layers):
            lifted[t, q, pl.ds(0, rows - px), :] = blank
            lifted[t, q, pl.ds(rows, rows - px), :] = blank

    chunk = max(d for d in range(1, 7) if slots % d == 0)
    fine_chunk = 2 if chunk % 2 == 0 else 1
    width = fine_chunk * px
    runs = slots // chunk

    for it in range(ITERS):
        forth, back = (2, 1) if it == ITERS - 1 else (3, 2)

        def cut_away(t):
            if it > 0:
                patch_copy(t).wait_send()
            done = cut(it, t, other, slots + t)
            for q in range(2 * layers):
                away[q // 2, q % 2 * px : (q % 2 + 1) * px, lanes(t, px)] = done[q * px : (q + 1) * px]
            patch_copy(t).start()

        def cut_own(t):
            done = cut(it, t, core, t)
            for q in range(2 * layers):
                patches[core * layers + q // 2, q % 2 * px : (q % 2 + 1) * px, lanes(t, px)] = (
                    done[q * px : (q + 1) * px]
                )

        loop(slots, cut_away)
        loop(slots, cut_own)
        if it == 0:
            loop(slots, build_put)
        if it > 0:
            whole_sum(it - 1)
            finish_probe(it - 1)
        loop(slots, lambda t: patch_copy(t).wait_recv())

        def wait_patterns():
            def arrive(i, carry):
                @pl.when(core * half + i != ix)
                def _():
                    pattern_copy(ix, i).wait_recv()

                return carry

            lax.fori_loop(0, half, arrive, 0)

        if it == 0:
            tabs_load.wait()
            for copy in probe_loads:
                copy.wait()
            if runs > 8:
                wait_patterns()

        pg_sum[...] = jnp.zeros_like(pg_sum)

        def run(k):
            first = k * chunk
            spans = [lanes(first // fine_chunk + i, width) for i in range(chunk // fine_chunk)]
            w = jnp.concatenate([wave[...]] * fine_chunk, axis=1)
            psi = [times(w, patches[0, :, span].astype(F32), px) for span in spans]
            for l in range(1, total):
                for i, span in enumerate(spans):
                    phi = both_sides(psi[i], tabs, 0, 1, px, forth)
                    phis[l - 1, :, span] = phi
                    psi[i] = times(phi, patches[l, :, span].astype(F32), px)
            if it == 0 and runs <= 8 and k == 0:
                wait_patterns()
            g = []
            for i in range(len(spans)):
                far = both_sides(psi[i], tabs, 2, 3, px, forth)
                target = []
                for s in range(fine_chunk):
                    t = first + i * fine_chunk + s
                    target.append(pat[t // cap, t % cap].astype(F32))
                target = jnp.concatenate(target, axis=1)
                fr, fi = far[:px], far[px:]
                miss = jnp.where(target >= 0.0, 2.0 * (fr * fr + fi * fi - target), 0.0)
                g.append(jnp.concatenate([miss * fr, miss * fi], axis=0))
            g = [both_sides(one, tabs, 3, 2, px, back) for one in g]
            for l in range(total - 1, -1, -1):
                for i, span in enumerate(spans):
                    before = phis[l - 1, :, span] if l else w
                    grads[l, :, span] = conj_times(before, g[i], px).astype(BF16)
                    g[i] = conj_times(patches[l, :, span].astype(F32), g[i], px)
                    if l:
                        g[i] = both_sides(g[i], tabs, 1, 0, px, back)
            for one in g:
                for s in range(fine_chunk):
                    pg_sum[...] += one[:, s * px : (s + 1) * px]

        if it > 0:
            grad_copy(it - 1).wait_send()
        loop(runs, run)

        pg_mine[it] = pg_sum[...].astype(BF16)
        for d in range(1, plane):
            piece_copy(it, d).start()
        grad_copy(it).start()

        def place(source, first, base, c, last):
            def lift(t):
                for q in range(2 * layers):
                    lifted[t, q, pl.ds(rows - px, px), :] = (
                        source[first + q // 2, q % 2 * px : (q % 2 + 1) * px, lanes(t, px)].astype(F32)
                    )

            def spread(t):
                row, _ = slot_corner(t, c)
                for q in range(2 * layers):
                    placed[q, :, lanes(base + t, px)] = lifted[t, q, pl.ds(rows - px - row, rows), :].astype(BF16)

            loop(slots, lift)
            loop(slots, spread)
            span = pl.ds(base * px, slots * px)
            for q in range(2 * layers):
                add = STEP_OBJECT * dot(placed[q, :, span], put_c[span, :])
                for j in range(cols // px):
                    now = field[q, j] - add[:, j * px : (j + 1) * px]
                    if last:
                        obj_out[q // 2, q % 2, :, lanes(j, px)] = now
                    else:
                        field[q, j] = now

        place(grads, core * layers, 0, core, False)
        plane_sum(it)
        grad_copy(it).wait_recv()
        place(g_recv, 0, slots, other, it == ITERS - 1)

    whole_sum(ITERS - 1)
    finish_probe(ITERS - 1)
    probe_out[0] = wave[:px]
    probe_out[1] = wave[px:]

    @pl.when(mine_sends)
    def _():
        for d in range(1, n_tx):
            pattern_copy(along(d)[0], local_s).wait_send()

    loop(slots, lambda t: patch_copy(t).wait_send())
    grad_copy(ITERS - 1).wait_send()
    for it in range(ITERS):
        for d in range(1, plane):
            piece_copy(it, d).wait_send()
        for d in range(1, n_tx):
            zone_copy(it, d).wait_send()
        delta_copy(it).wait_send()


def body(object_field, probe_wave, measured, owner_row, list_rows, list_cols):
    layers, _, rows, cols = object_field.shape
    positions, px, _ = measured.shape
    n_tx, n_ty, n_sl = lax.axis_size("tx"), lax.axis_size("ty"), lax.axis_size("sl")
    cap = list_rows.shape[-1]
    half = n_tx // n_sl
    slots = half * cap
    total = n_sl * layers
    plane = n_ty * n_sl
    deep = 2 * px // n_sl
    tabs = jnp.asarray(real_tables(px))
    tables = [jnp.transpose(one, (0, 3, 1, 2)).reshape(cap, 1, n_tx) for one in (list_rows, list_cols)]
    vmem = pl.BlockSpec(memory_space=pltpu.VMEM)
    anywhere = pl.BlockSpec(memory_space=pl.ANY)
    smem = pl.BlockSpec(memory_space=pltpu.SMEM)
    dma = pltpu.SemaphoreType.DMA
    return pl.pallas_call(
        functools.partial(kernel, n_tx, n_ty, n_sl, cap, positions * n_tx * n_ty),
        out_shape=(
            pltpu.VMEM(object_field.shape, F32),
            pltpu.VMEM(probe_wave.shape, F32),
        ),
        in_specs=[anywhere, anywhere, anywhere, smem, smem, smem, anywhere],
        out_specs=(vmem, vmem),
        scratch_shapes=[
            pltpu.VMEM((2 * layers, cols // px, rows, px), F32),
            pltpu.VMEM(measured.shape, F32),
            pltpu.VMEM(tabs.shape, BF16),
            pltpu.VMEM((half, cap, px, px), BF16),
            pltpu.VMEM((n_tx, cap, px, px), BF16),
            pltpu.VMEM((2 * slots, 2 * px, px), BF16),
            pltpu.VMEM((2 * slots * px, cols), BF16),
            pltpu.VMEM((total, 2 * px, slots * px), BF16),
            pltpu.VMEM((layers, 2 * px, slots * px), BF16),
            pltpu.VMEM((total - 1, 2 * px, slots * px), F32),
            pltpu.VMEM((total, 2 * px, slots * px), BF16),
            pltpu.VMEM((layers, 2 * px, slots * px), BF16),
            pltpu.VMEM((slots, 2 * layers, 2 * rows - px, px), F32),
            pltpu.VMEM((2 * layers, rows, 2 * slots * px), BF16),
            pltpu.VMEM((ITERS, plane, deep, px), BF16),
            pltpu.VMEM((ITERS, 2 * px, px), BF16),
            pltpu.VMEM((ITERS, n_tx, deep, px), BF16),
            pltpu.VMEM((ITERS, 2 * px, px), F32),
            pltpu.VMEM((2 * px, px), F32),
            pltpu.VMEM((2 * px, px), F32),
            dma((2 * layers, cols // px)),
            dma((4,)),
            dma((n_tx,)),
            dma((half,)),
            dma((slots,)),
            dma((slots,)),
            dma((ITERS,)),
            dma((ITERS,)),
            dma((ITERS, plane)),
            dma((ITERS, plane)),
            dma((ITERS, n_tx)),
            dma((ITERS, n_tx)),
            dma((ITERS,)),
            dma((ITERS,)),
        ],
        compiler_params=pltpu.CompilerParams(
            collective_id=0, has_side_effects=True, vmem_limit_bytes=58 * 2**20
        ),
    )(object_field, probe_wave, measured, *tables, owner_row.reshape(1, -1), tabs)


def solution(mesh):
    in_specs = (
        P(("groups", "sl"), None, "tx", "ty"),
        P("groups", None, None),
        P(("groups", "tx", "ty"), None, None),
        P(("groups", "tx", "ty"), None),
        P(("groups", "tx"), "ty", None, None),
        P(("groups", "tx"), "ty", None, None),
    )
    out_specs = (P(("groups", "sl"), None, "tx", "ty"), P("groups", None, None))
    return jax.shard_map(body, mesh=mesh, in_specs=in_specs, out_specs=out_specs, check_vma=False)
```

```python
import functools
import math

import jax
import jax.numpy as jnp
import numpy as np
from jax import lax
from jax.experimental import pallas as pl
from jax.experimental.pallas import tpu as pltpu
from jax.sharding import PartitionSpec as P

ITERS = 2
PHASE = 0.25
STEP_OBJECT = 0.01
STEP_PROBE = 0.6
KERN_SCALE = 1.6465
F32 = jnp.float32
BF16 = jnp.bfloat16
MESH = pl.DeviceIdType.MESH


def real_tables(pixels):
    index = np.arange(pixels)
    four = np.exp(-2j * math.pi * ((index[:, None] * index[None, :]) % pixels) / pixels) / math.sqrt(pixels)
    freq = np.where(index < pixels // 2, index, index - pixels).astype(np.float64)
    kern = (np.conj(four) * np.exp(-1j * PHASE * freq * freq / pixels)[None, :]) @ four
    found = []
    for matrix in (KERN_SCALE * kern, math.sqrt(pixels) * four):
        right = np.block([[matrix.real, matrix.imag], [-matrix.imag, matrix.real]])
        found += [right, right.T]
    whole = np.stack(found).astype(np.float32)
    high = whole.astype(jnp.bfloat16)
    low = (whole - high.astype(np.float32)).astype(jnp.bfloat16)
    return np.stack([high, low], axis=1)


def split(x):
    high = x.astype(BF16)
    return high, (x - high.astype(F32)).astype(BF16)


def dot(a, b):
    return jnp.dot(a, b, preferred_element_type=F32)


def loop(count, step):
    if count <= 8:
        for i in range(count):
            step(i)
    else:
        lax.fori_loop(0, count, lambda i, carry: (step(i), carry)[1], 0)


def lanes(i, width):
    return pl.ds(i * width if isinstance(i, int) else pl.multiple_of(i * width, width), width)


def both_sides(x, tabs, right, left, px, passes):
    count = x.shape[1] // px
    scale = 1.0 / px if right >= 2 else KERN_SCALE**-2

    def rows(v):
        return jnp.concatenate(
            [
                jnp.concatenate([v[:px, s * px : (s + 1) * px], v[px:, s * px : (s + 1) * px]], axis=1)
                for s in range(count)
            ],
            axis=0,
        )

    def columns(v):
        return jnp.concatenate(
            [
                jnp.concatenate([v[s * px : (s + 1) * px, :px], v[s * px : (s + 1) * px, px:]], axis=0)
                for s in range(count)
            ],
            axis=1,
        )

    m_high, m_low = tabs[right, 0], tabs[right, 1]
    n_high, n_low = tabs[left, 0], tabs[left, 1]
    if passes == 1:
        y = dot(rows(x.astype(BF16)), m_high)
        return scale * dot(n_high, columns(y.astype(BF16)))
    if passes == 2:
        v = rows(x.astype(BF16))
        y = dot(jnp.concatenate([v, v], axis=1), jnp.concatenate([m_high, m_low], axis=0))
        v = columns(y.astype(BF16))
        return scale * dot(jnp.concatenate([n_high, n_low], axis=1), jnp.concatenate([v, v], axis=0))
    high, low = split(x)
    high, low = rows(high), rows(low)
    y = dot(
        jnp.concatenate([high, low, high], axis=1), jnp.concatenate([m_high, m_high, m_low], axis=0)
    )
    high, low = split(y)
    high, low = columns(high), columns(low)
    return scale * dot(
        jnp.concatenate([n_high, n_high, n_low], axis=1), jnp.concatenate([high, low, high], axis=0)
    )


def times(a, b, px):
    ar, ai, br, bi = a[:px], a[px:], b[:px], b[px:]
    return jnp.concatenate([ar * br - ai * bi, ar * bi + ai * br], axis=0)


def conj_times(a, g, px):
    ar, ai, gr, gi = a[:px], a[px:], g[:px], g[px:]
    return jnp.concatenate([ar * gr + ai * gi, ar * gi - ai * gr], axis=0)


def kernel(
    n_tx, n_ty, n_sl, cap, all_positions,
    obj, probe, measured_at, list_r_at, list_c_at, owner_at, tabs_at,
    obj_out, probe_out,
    list_r, list_c, owner, field, measured, tabs, pat, staged, cut_c, put_c, patches, away, phis, grads, g_recv, lifted, placed,
    pieces, pg_mine, zone, deltas, wave, pg_sum,
    load_sem, in_sem, pat_send, pat_recv, p_send, p_recv, g_send, g_rcv, pc_send, pc_recv, zn_send, zn_recv, dl_send, dl_recv,
):
    ix, iy, core = lax.axis_index("tx"), lax.axis_index("ty"), lax.axis_index("sl")
    layers, _, rows, cols = obj.shape
    positions, px, _ = measured.shape
    half = n_tx // n_sl
    slots = half * cap
    total = n_sl * layers
    other = 1 - core
    plane = n_ty * n_sl
    flat = iy * n_sl + core
    deep = 2 * px // n_sl
    peer = {"sl": other}

    def beside(d):
        i = lax.rem(flat + d, plane)
        return i, {"ty": i // n_sl, "sl": lax.rem(i, n_sl)}

    def along(d):
        i = lax.rem(ix + d, n_tx)
        return i, {"tx": i}

    barrier = pltpu.get_barrier_semaphore()
    for d in range(1, plane):
        pl.semaphore_signal(barrier, inc=1, device_id=beside(d)[1], device_id_type=MESH)
    for d in range(1, n_tx):
        pl.semaphore_signal(barrier, inc=1, device_id=along(d)[1], device_id_type=MESH)

    routing = [
        pltpu.make_async_copy(source, kept, in_sem.at[4 + i])
        for i, (source, kept) in enumerate(((list_c_at, list_c), (owner_at, owner), (list_r_at, list_r)))
    ]
    for copy in routing:
        copy.start()

    def load(q):
        return [
            pltpu.make_async_copy(obj.at[q // 2, q % 2, :, lanes(j, px)], field.at[q, j], load_sem.at[q, j])
            for j in range(cols // px)
        ]

    for q in range(2 * layers):
        for copy in load(q):
            copy.start()

    measured_load = pltpu.make_async_copy(measured_at, measured, in_sem.at[0])
    tabs_load = pltpu.make_async_copy(tabs_at, tabs, in_sem.at[1])
    measured_load.start()
    tabs_load.start()
    probe_loads = [
        pltpu.make_async_copy(probe.at[part], wave.at[pl.ds(part * px, px)], in_sem.at[2 + part]) for part in range(2)
    ]
    for copy in probe_loads:
        copy.start()


    def stage(o, carry):
        seen = jnp.int32(0)
        found = [jnp.int32(-1)] * cap
        for p in range(positions):
            here = owner[0, p] == o
            for k in range(cap):
                found[k] = jnp.where(here & (seen == k), jnp.int32(p), found[k])
            seen = seen + jnp.where(here, 1, 0)
        for k in range(cap):
            values = jnp.full((px, px), -1.0, F32)
            for p in range(positions):
                values = jnp.where(found[k] == p, measured[p], values)
            staged[o, k] = values.astype(BF16)
        return carry


    def slot_corner(t, c):
        s, k = c * half + t // cap, t % cap
        return jnp.clip(list_r[k, 0, s], 0, rows - px), jnp.clip(list_c[k, 0, s], 0, cols - px)

    def hot(shape, axis, shift):
        long = lax.broadcasted_iota(jnp.int32, shape, axis)
        short = lax.broadcasted_iota(jnp.int32, shape, 1 - axis)
        return jnp.where(long - short == shift, 1.0, 0.0).astype(BF16)

    def column_block(col):
        return jnp.minimum(col // px, cols // px - 2)

    def build_cut(t):
        for at, c in ((t, core), (slots + t, other)):
            _, col = slot_corner(t, c)
            cut_c[at] = hot((2 * px, px), 0, col - column_block(col) * px)

    for copy in routing:
        copy.wait()
    loop(slots, build_cut)
    measured_load.wait()
    lax.fori_loop(0, n_tx, stage, 0)
    for q in range(2 * layers):
        for copy in load(q):
            copy.wait()
    pl.semaphore_wait(barrier, plane - 1 + n_tx - 1)

    mine_sends = (ix // half) == core
    local_s = lax.rem(ix, half)

    def pattern_copy(o, s):
        return pltpu.make_async_remote_copy(
            src_ref=staged.at[o], dst_ref=pat.at[s], send_sem=pat_send.at[o], recv_sem=pat_recv.at[s],
            device_id={"tx": o}, device_id_type=MESH,
        )

    @pl.when(mine_sends)
    def _():
        for d in range(n_tx - 1, 0, -1):
            pattern_copy(along(d)[0], local_s).start()
        pat[local_s] = staged[ix]

    def patch_copy(t):
        return pltpu.make_async_remote_copy(
            src_ref=away.at[:, :, lanes(t, px)],
            dst_ref=patches.at[pl.ds(core * layers, layers), :, lanes(t, px)],
            send_sem=p_send.at[t], recv_sem=p_recv.at[t], device_id=peer, device_id_type=MESH,
        )

    def grad_copy(it):
        return pltpu.make_async_remote_copy(
            src_ref=grads.at[pl.ds(other * layers, layers)], dst_ref=g_recv,
            send_sem=g_send.at[it], recv_sem=g_rcv.at[it], device_id=peer, device_id_type=MESH,
        )

    own_rows = pl.ds(pl.multiple_of(core * deep, deep), deep)

    def piece_copy(it, d):
        i, where = beside(d)
        theirs = pl.ds(pl.multiple_of(lax.rem(i, n_sl) * deep, deep), deep)
        return pltpu.make_async_remote_copy(
            src_ref=pg_mine.at[it, theirs], dst_ref=pieces.at[it, flat],
            send_sem=pc_send.at[it, d], recv_sem=pc_recv.at[it, d], device_id=where, device_id_type=MESH,
        )

    def zone_copy(it, d):
        return pltpu.make_async_remote_copy(
            src_ref=zone.at[it, ix], dst_ref=zone.at[it, ix],
            send_sem=zn_send.at[it, d], recv_sem=zn_recv.at[it, d], device_id=along(d)[1], device_id_type=MESH,
        )

    def delta_copy(it):
        return pltpu.make_async_remote_copy(
            src_ref=deltas.at[it, own_rows], dst_ref=deltas.at[it, own_rows],
            send_sem=dl_send.at[it], recv_sem=dl_recv.at[it], device_id=peer, device_id_type=MESH,
        )

    def plane_sum(it):
        pieces[it, flat] = pg_mine[it, own_rows]
        for d in range(1, plane):
            piece_copy(it, d).wait_recv()
        add = pieces[it, 0].astype(F32)
        for i in range(1, plane):
            add = add + pieces[it, i].astype(F32)
        zone[it, ix] = add.astype(BF16)
        for d in range(1, n_tx):
            zone_copy(it, d).start()

    def whole_sum(it):
        for d in range(1, n_tx):
            zone_copy(it, d).wait_recv()
        add = zone[it, 0].astype(F32)
        for i in range(1, n_tx):
            add = add + zone[it, i].astype(F32)
        deltas[it, own_rows] = add
        delta_copy(it).start()

    def finish_probe(it):
        delta_copy(it).wait_recv()
        wave[...] -= (STEP_PROBE / all_positions) * deltas[it]

    def cut(it, t, c, at):
        row, col = slot_corner(t, c)
        first = column_block(col)
        held = jnp.concatenate(
            [
                jnp.concatenate(
                    [field[q, first + j, pl.ds(row, px), :].astype(BF16) for j in range(2)], axis=1
                )
                for q in range(2 * layers)
            ],
            axis=0,
        )
        return dot(held, cut_c[at]).astype(BF16)

    def build_put(t):
        _, col = slot_corner(t, core)
        put_c[lanes(t, px), :] = hot((px, cols), 1, col)
        _, col = slot_corner(t, other)
        put_c[lanes(slots + t, px), :] = hot((px, cols), 1, col)
        blank = jnp.zeros((rows - px, px), F32)
        for q in range(2 * layers):
            lifted[t, q, pl.ds(0, rows - px), :] = blank
            lifted[t, q, pl.ds(rows, rows - px), :] = blank

    chunk = max(d for d in range(1, 7) if slots % d == 0)
    fine_chunk = 2 if chunk % 2 == 0 else 1
    width = fine_chunk * px
    runs = slots // chunk

    for it in range(ITERS):
        forth, back = (2, 1) if it == ITERS - 1 else (3, 2)

        def cut_away(t):
            if it > 0:
                patch_copy(t).wait_send()
            done = cut(it, t, other, slots + t)
            for q in range(2 * layers):
                away[q // 2, q % 2 * px : (q % 2 + 1) * px, lanes(t, px)] = done[q * px : (q + 1) * px]
            patch_copy(t).start()

        def cut_own(t):
            done = cut(it, t, core, t)
            for q in range(2 * layers):
                patches[core * layers + q // 2, q % 2 * px : (q % 2 + 1) * px, lanes(t, px)] = (
                    done[q * px : (q + 1) * px]
                )

        loop(slots, cut_away)
        loop(slots, cut_own)
        if it > 0:
            whole_sum(it - 1)
            finish_probe(it - 1)
        loop(slots, lambda t: patch_copy(t).wait_recv())

        def wait_patterns():
            def arrive(i, carry):
                @pl.when(core * half + i != ix)
                def _():
                    pattern_copy(ix, i).wait_recv()

                return carry

            lax.fori_loop(0, half, arrive, 0)

        if it == 0:
            tabs_load.wait()
            for copy in probe_loads:
                copy.wait()
            if runs > 8:
                wait_patterns()

        if runs > 1:
            pg_sum[...] = jnp.zeros_like(pg_sum)

        def run(k):
            first = k * chunk
            spans = [lanes(first // fine_chunk + i, width) for i in range(chunk // fine_chunk)]
            w = jnp.concatenate([wave[...]] * fine_chunk, axis=1)
            psi = [times(w, patches[0, :, span].astype(F32), px) for span in spans]
            for l in range(1, total):
                for i, span in enumerate(spans):
                    phi = both_sides(psi[i], tabs, 0, 1, px, forth)
                    phis[l - 1, :, span] = phi
                    psi[i] = times(phi, patches[l, :, span].astype(F32), px)
            if it == 0 and runs <= 8 and k == 0:
                wait_patterns()
            g = []
            for i in range(len(spans)):
                far = both_sides(psi[i], tabs, 2, 3, px, forth)
                target = []
                for s in range(fine_chunk):
                    t = first + i * fine_chunk + s
                    target.append(pat[t // cap, t % cap].astype(F32))
                target = jnp.concatenate(target, axis=1)
                fr, fi = far[:px], far[px:]
                miss = jnp.where(target >= 0.0, 2.0 * (fr * fr + fi * fi - target), 0.0)
                g.append(jnp.concatenate([miss * fr, miss * fi], axis=0))
            g = [both_sides(one, tabs, 3, 2, px, back) for one in g]
            for l in range(total - 1, -1, -1):
                for i, span in enumerate(spans):
                    before = phis[l - 1, :, span] if l else w
                    grads[l, :, span] = conj_times(before, g[i], px).astype(BF16)
                    g[i] = conj_times(patches[l, :, span].astype(F32), g[i], px)
                    if l:
                        g[i] = both_sides(g[i], tabs, 1, 0, px, back)
            add = None
            for one in g:
                for s in range(fine_chunk):
                    part = one[:, s * px : (s + 1) * px]
                    add = part if add is None else add + part
            if runs == 1:
                pg_mine[it] = add.astype(BF16)
            else:
                pg_sum[...] += add

        if it > 0:
            grad_copy(it - 1).wait_send()
        loop(runs, run)

        if runs > 1:
            pg_mine[it] = pg_sum[...].astype(BF16)
        for d in range(1, plane):
            piece_copy(it, d).start()
        grad_copy(it).start()
        if it == 0:
            loop(slots, build_put)

        def place(source, first, base, c, last):
            def lift(t):
                for q in range(2 * layers):
                    lifted[t, q, pl.ds(rows - px, px), :] = (
                        source[first + q // 2, q % 2 * px : (q % 2 + 1) * px, lanes(t, px)].astype(F32)
                    )

            def spread(t):
                row, _ = slot_corner(t, c)
                for q in range(2 * layers):
                    placed[q, :, lanes(base + t, px)] = lifted[t, q, pl.ds(rows - px - row, rows), :].astype(BF16)

            loop(slots, lift)
            loop(slots, spread)
            span = pl.ds(base * px, slots * px)
            for q in range(2 * layers):
                add = STEP_OBJECT * dot(placed[q, :, span], put_c[span, :])
                for j in range(cols // px):
                    now = field[q, j] - add[:, j * px : (j + 1) * px]
                    if last:
                        obj_out[q // 2, q % 2, :, lanes(j, px)] = now
                    else:
                        field[q, j] = now

        place(grads, core * layers, 0, core, False)
        plane_sum(it)
        grad_copy(it).wait_recv()
        place(g_recv, 0, slots, other, it == ITERS - 1)

    whole_sum(ITERS - 1)
    finish_probe(ITERS - 1)
    probe_out[0] = wave[:px]
    probe_out[1] = wave[px:]

    @pl.when(mine_sends)
    def _():
        for d in range(1, n_tx):
            pattern_copy(along(d)[0], local_s).wait_send()

    loop(slots, lambda t: patch_copy(t).wait_send())
    grad_copy(ITERS - 1).wait_send()
    for it in range(ITERS):
        for d in range(1, plane):
            piece_copy(it, d).wait_send()
        for d in range(1, n_tx):
            zone_copy(it, d).wait_send()
        delta_copy(it).wait_send()


def body(object_field, probe_wave, measured, owner_row, list_rows, list_cols):
    layers, _, rows, cols = object_field.shape
    positions, px, _ = measured.shape
    n_tx, n_ty, n_sl = lax.axis_size("tx"), lax.axis_size("ty"), lax.axis_size("sl")
    cap = list_rows.shape[-1]
    half = n_tx // n_sl
    slots = half * cap
    total = n_sl * layers
    plane = n_ty * n_sl
    deep = 2 * px // n_sl
    tabs = jnp.asarray(real_tables(px))
    tables = [jnp.transpose(one, (0, 3, 1, 2)).reshape(cap, 1, n_tx) for one in (list_rows, list_cols)]
    vmem = pl.BlockSpec(memory_space=pltpu.VMEM)
    anywhere = pl.BlockSpec(memory_space=pl.ANY)
    dma = pltpu.SemaphoreType.DMA
    return pl.pallas_call(
        functools.partial(kernel, n_tx, n_ty, n_sl, cap, positions * n_tx * n_ty),
        out_shape=(
            pltpu.VMEM(object_field.shape, F32),
            pltpu.VMEM(probe_wave.shape, F32),
        ),
        in_specs=[anywhere, anywhere, anywhere, anywhere, anywhere, anywhere, anywhere],
        out_specs=(vmem, vmem),
        scratch_shapes=[
            pltpu.SMEM(tables[0].shape, jnp.int32),
            pltpu.SMEM(tables[1].shape, jnp.int32),
            pltpu.SMEM((1, positions), jnp.int32),
            pltpu.VMEM((2 * layers, cols // px, rows, px), F32),
            pltpu.VMEM(measured.shape, F32),
            pltpu.VMEM(tabs.shape, BF16),
            pltpu.VMEM((half, cap, px, px), BF16),
            pltpu.VMEM((n_tx, cap, px, px), BF16),
            pltpu.VMEM((2 * slots, 2 * px, px), BF16),
            pltpu.VMEM((2 * slots * px, cols), BF16),
            pltpu.VMEM((total, 2 * px, slots * px), BF16),
            pltpu.VMEM((layers, 2 * px, slots * px), BF16),
            pltpu.VMEM((total - 1, 2 * px, slots * px), F32),
            pltpu.VMEM((total, 2 * px, slots * px), BF16),
            pltpu.VMEM((layers, 2 * px, slots * px), BF16),
            pltpu.VMEM((slots, 2 * layers, 2 * rows - px, px), F32),
            pltpu.VMEM((2 * layers, rows, 2 * slots * px), BF16),
            pltpu.VMEM((ITERS, plane, deep, px), BF16),
            pltpu.VMEM((ITERS, 2 * px, px), BF16),
            pltpu.VMEM((ITERS, n_tx, deep, px), BF16),
            pltpu.VMEM((ITERS, 2 * px, px), F32),
            pltpu.VMEM((2 * px, px), F32),
            pltpu.VMEM((2 * px, px), F32),
            dma((2 * layers, cols // px)),
            dma((7,)),
            dma((n_tx,)),
            dma((half,)),
            dma((slots,)),
            dma((slots,)),
            dma((ITERS,)),
            dma((ITERS,)),
            dma((ITERS, plane)),
            dma((ITERS, plane)),
            dma((ITERS, n_tx)),
            dma((ITERS, n_tx)),
            dma((ITERS,)),
            dma((ITERS,)),
        ],
        compiler_params=pltpu.CompilerParams(
            collective_id=0, has_side_effects=True, vmem_limit_bytes=58 * 2**20
        ),
    )(object_field, probe_wave, measured, *tables, owner_row.reshape(1, -1), tabs)


def solution(mesh):
    in_specs = (
        P(("groups", "sl"), None, "tx", "ty"),
        P("groups", None, None),
        P(("groups", "tx", "ty"), None, None),
        P(("groups", "tx", "ty"), None),
        P(("groups", "tx"), "ty", None, None),
        P(("groups", "tx"), "ty", None, None),
    )
    out_specs = (P(("groups", "sl"), None, "tx", "ty"), P("groups", None, None))
    return jax.shard_map(body, mesh=mesh, in_specs=in_specs, out_specs=out_specs, check_vma=False)
```

```python
import functools
import math

import jax
import jax.numpy as jnp
import numpy as np
from jax import lax
from jax.experimental import pallas as pl
from jax.experimental.pallas import tpu as pltpu
from jax.sharding import PartitionSpec as P

ITERS = 2
PHASE = 0.25
STEP_OBJECT = 0.01
STEP_PROBE = 0.6
KERN_SCALE = 1.6465
F32 = jnp.float32
BF16 = jnp.bfloat16
MESH = pl.DeviceIdType.MESH


def real_tables(pixels):
    index = np.arange(pixels)
    four = np.exp(-2j * math.pi * ((index[:, None] * index[None, :]) % pixels) / pixels) / math.sqrt(pixels)
    freq = np.where(index < pixels // 2, index, index - pixels).astype(np.float64)
    kern = (np.conj(four) * np.exp(-1j * PHASE * freq * freq / pixels)[None, :]) @ four
    found = []
    for matrix in (KERN_SCALE * kern, math.sqrt(pixels) * four):
        right = np.block([[matrix.real, matrix.imag], [-matrix.imag, matrix.real]])
        found += [right, right.T]
    whole = np.stack(found).astype(np.float32)
    high = whole.astype(jnp.bfloat16)
    low = (whole - high.astype(np.float32)).astype(jnp.bfloat16)
    return np.stack([high, low], axis=1)


def split(x):
    high = x.astype(BF16)
    return high, (x - high.astype(F32)).astype(BF16)


def dot(a, b):
    return jnp.dot(a, b, preferred_element_type=F32)


def loop(count, step):
    if count <= 8:
        for i in range(count):
            step(i)
    else:
        lax.fori_loop(0, count, lambda i, carry: (step(i), carry)[1], 0)


def lanes(i, width):
    return pl.ds(i * width if isinstance(i, int) else pl.multiple_of(i * width, width), width)


def both_sides(x, tabs, right, left, px, passes):
    count = x.shape[1] // px
    scale = 1.0 / px if right >= 2 else KERN_SCALE**-2

    def rows(v):
        return jnp.concatenate(
            [
                jnp.concatenate([v[:px, s * px : (s + 1) * px], v[px:, s * px : (s + 1) * px]], axis=1)
                for s in range(count)
            ],
            axis=0,
        )

    def columns(v):
        return jnp.concatenate(
            [
                jnp.concatenate([v[s * px : (s + 1) * px, :px], v[s * px : (s + 1) * px, px:]], axis=0)
                for s in range(count)
            ],
            axis=1,
        )

    m_high, m_low = tabs[right, 0], tabs[right, 1]
    n_high, n_low = tabs[left, 0], tabs[left, 1]
    if passes == 1:
        y = dot(rows(x.astype(BF16)), m_high)
        return scale * dot(n_high, columns(y.astype(BF16)))
    if passes == 2:
        v = rows(x.astype(BF16))
        y = dot(jnp.concatenate([v, v], axis=1), jnp.concatenate([m_high, m_low], axis=0))
        v = columns(y.astype(BF16))
        return scale * dot(jnp.concatenate([n_high, n_low], axis=1), jnp.concatenate([v, v], axis=0))
    high, low = split(x)
    high, low = rows(high), rows(low)
    y = dot(
        jnp.concatenate([high, low, high], axis=1), jnp.concatenate([m_high, m_high, m_low], axis=0)
    )
    high, low = split(y)
    high, low = columns(high), columns(low)
    return scale * dot(
        jnp.concatenate([n_high, n_high, n_low], axis=1), jnp.concatenate([high, low, high], axis=0)
    )


def times(a, b, px):
    ar, ai, br, bi = a[:px], a[px:], b[:px], b[px:]
    return jnp.concatenate([ar * br - ai * bi, ar * bi + ai * br], axis=0)


def conj_times(a, g, px):
    ar, ai, gr, gi = a[:px], a[px:], g[:px], g[px:]
    return jnp.concatenate([ar * gr + ai * gi, ar * gi - ai * gr], axis=0)


def kernel(
    n_tx, n_ty, n_sl, cap, all_positions,
    obj, probe, measured_at, list_r_at, list_c_at, owner_at, tabs_at,
    obj_out, probe_out,
    list_r, list_c, owner, field, measured, tabs, pat, staged, cut_c, put_c, patches, away, phis, grads, g_recv, lifted, placed,
    pieces, pg_mine, zone, deltas, wave, pg_sum,
    load_sem, in_sem, pat_send, pat_recv, p_send, p_recv, g_send, g_rcv, pc_send, pc_recv, zn_send, zn_recv, dl_send, dl_recv,
):
    ix, iy, core = lax.axis_index("tx"), lax.axis_index("ty"), lax.axis_index("sl")
    layers, _, rows, cols = obj.shape
    positions, px, _ = measured.shape
    half = n_tx // n_sl
    slots = half * cap
    total = n_sl * layers
    other = 1 - core
    plane = n_ty * n_sl
    flat = iy * n_sl + core
    deep = 2 * px // n_sl
    peer = {"sl": other}

    def beside(d):
        i = lax.rem(flat + d, plane)
        return i, {"ty": i // n_sl, "sl": lax.rem(i, n_sl)}

    def along(d):
        i = lax.rem(ix + d, n_tx)
        return i, {"tx": i}

    barrier = pltpu.get_barrier_semaphore()
    for d in range(1, plane):
        pl.semaphore_signal(barrier, inc=1, device_id=beside(d)[1], device_id_type=MESH)
    for d in range(1, n_tx):
        pl.semaphore_signal(barrier, inc=1, device_id=along(d)[1], device_id_type=MESH)

    routing = [
        pltpu.make_async_copy(source, kept, in_sem.at[4 + i])
        for i, (source, kept) in enumerate(((list_c_at, list_c), (owner_at, owner), (list_r_at, list_r)))
    ]
    for copy in routing:
        copy.start()

    def load(q):
        return [
            pltpu.make_async_copy(obj.at[q // 2, q % 2, :, lanes(j, px)], field.at[q, j], load_sem.at[q, j])
            for j in range(cols // px)
        ]

    for q in range(2 * layers):
        for copy in load(q):
            copy.start()

    measured_load = pltpu.make_async_copy(measured_at, measured, in_sem.at[0])
    tabs_load = pltpu.make_async_copy(tabs_at, tabs, in_sem.at[1])
    measured_load.start()
    tabs_load.start()
    probe_loads = [
        pltpu.make_async_copy(probe.at[part], wave.at[pl.ds(part * px, px)], in_sem.at[2 + part]) for part in range(2)
    ]
    for copy in probe_loads:
        copy.start()


    def stage(o, carry):
        seen = jnp.int32(0)
        found = [jnp.int32(-1)] * cap
        for p in range(positions):
            here = owner[0, p] == o
            for k in range(cap):
                found[k] = jnp.where(here & (seen == k), jnp.int32(p), found[k])
            seen = seen + jnp.where(here, 1, 0)
        for k in range(cap):
            values = jnp.full((px, px), -1.0, F32)
            for p in range(positions):
                values = jnp.where(found[k] == p, measured[p], values)
            staged[o, k] = values.astype(BF16)
        return carry


    def slot_corner(t, c):
        s, k = c * half + t // cap, t % cap
        return jnp.clip(list_r[k, 0, s], 0, rows - px), jnp.clip(list_c[k, 0, s], 0, cols - px)

    def hot(shape, axis, shift):
        long = lax.broadcasted_iota(jnp.int32, shape, axis)
        short = lax.broadcasted_iota(jnp.int32, shape, 1 - axis)
        return jnp.where(long - short == shift, 1.0, 0.0).astype(BF16)

    def column_block(col):
        return jnp.minimum(col // px, cols // px - 2)

    def build_cut(t):
        for at, c in ((t, core), (slots + t, other)):
            _, col = slot_corner(t, c)
            cut_c[at] = hot((2 * px, px), 0, col - column_block(col) * px)

    for copy in routing:
        copy.wait()
    loop(slots, build_cut)
    measured_load.wait()
    lax.fori_loop(0, n_tx, stage, 0)
    for q in range(2 * layers):
        for copy in load(q):
            copy.wait()
    pl.semaphore_wait(barrier, plane - 1 + n_tx - 1)

    mine_sends = (ix // half) == core
    local_s = lax.rem(ix, half)

    def pattern_copy(o, s):
        return pltpu.make_async_remote_copy(
            src_ref=staged.at[o], dst_ref=pat.at[s], send_sem=pat_send.at[o], recv_sem=pat_recv.at[s],
            device_id={"tx": o}, device_id_type=MESH,
        )

    @pl.when(mine_sends)
    def _():
        for d in range(n_tx - 1, 0, -1):
            pattern_copy(along(d)[0], local_s).start()
        pat[local_s] = staged[ix]

    def patch_copy(t):
        return pltpu.make_async_remote_copy(
            src_ref=away.at[:, :, lanes(t, px)],
            dst_ref=patches.at[pl.ds(core * layers, layers), :, lanes(t, px)],
            send_sem=p_send.at[t], recv_sem=p_recv.at[t], device_id=peer, device_id_type=MESH,
        )

    def grad_copy(it):
        return pltpu.make_async_remote_copy(
            src_ref=grads.at[pl.ds(other * layers, layers)], dst_ref=g_recv,
            send_sem=g_send.at[it], recv_sem=g_rcv.at[it], device_id=peer, device_id_type=MESH,
        )

    own_rows = pl.ds(pl.multiple_of(core * deep, deep), deep)

    def piece_copy(it, d):
        i, where = beside(d)
        theirs = pl.ds(pl.multiple_of(lax.rem(i, n_sl) * deep, deep), deep)
        return pltpu.make_async_remote_copy(
            src_ref=pg_mine.at[it, theirs], dst_ref=pieces.at[it, flat],
            send_sem=pc_send.at[it, d], recv_sem=pc_recv.at[it, d], device_id=where, device_id_type=MESH,
        )

    def zone_copy(it, d):
        return pltpu.make_async_remote_copy(
            src_ref=zone.at[it, ix], dst_ref=zone.at[it, ix],
            send_sem=zn_send.at[it, d], recv_sem=zn_recv.at[it, d], device_id=along(d)[1], device_id_type=MESH,
        )

    def delta_copy(it):
        return pltpu.make_async_remote_copy(
            src_ref=deltas.at[it, own_rows], dst_ref=deltas.at[it, own_rows],
            send_sem=dl_send.at[it], recv_sem=dl_recv.at[it], device_id=peer, device_id_type=MESH,
        )

    def plane_sum(it):
        pieces[it, flat] = pg_mine[it, own_rows]
        for d in range(1, plane):
            piece_copy(it, d).wait_recv()
        add = pieces[it, 0].astype(F32)
        for i in range(1, plane):
            add = add + pieces[it, i].astype(F32)
        zone[it, ix] = add.astype(BF16)
        for d in range(1, n_tx):
            zone_copy(it, d).start()

    def whole_sum(it):
        for d in range(1, n_tx):
            zone_copy(it, d).wait_recv()
        add = zone[it, 0].astype(F32)
        for i in range(1, n_tx):
            add = add + zone[it, i].astype(F32)
        deltas[it, own_rows] = add
        delta_copy(it).start()

    def finish_probe(it):
        delta_copy(it).wait_recv()
        wave[...] -= (STEP_PROBE / all_positions) * deltas[it]

    def cut(it, t, c, at):
        row, col = slot_corner(t, c)
        first = column_block(col)
        held = jnp.concatenate(
            [
                jnp.concatenate(
                    [field[q, first + j, pl.ds(row, px), :].astype(BF16) for j in range(2)], axis=1
                )
                for q in range(2 * layers)
            ],
            axis=0,
        )
        return dot(held, cut_c[at]).astype(BF16)

    def build_put(t):
        _, col = slot_corner(t, core)
        put_c[lanes(t, px), :] = hot((px, cols), 1, col)
        _, col = slot_corner(t, other)
        put_c[lanes(slots + t, px), :] = hot((px, cols), 1, col)
        blank = jnp.zeros((rows - px, px), F32)
        for q in range(2 * layers):
            lifted[t, q, pl.ds(0, rows - px), :] = blank
            lifted[t, q, pl.ds(rows, rows - px), :] = blank

    chunk = max(d for d in range(1, 7) if slots % d == 0)
    fine_chunk = 2 if chunk % 2 == 0 else 1
    width = fine_chunk * px
    runs = slots // chunk

    for it in range(ITERS):
        forth, back = (2, 1) if it == ITERS - 1 else (3, 2)

        def cut_away(t):
            if it > 0:
                patch_copy(t).wait_send()
            done = cut(it, t, other, slots + t)
            for q in range(2 * layers):
                away[q // 2, q % 2 * px : (q % 2 + 1) * px, lanes(t, px)] = done[q * px : (q + 1) * px]
            patch_copy(t).start()

        def cut_own(t):
            done = cut(it, t, core, t)
            for q in range(2 * layers):
                patches[core * layers + q // 2, q % 2 * px : (q % 2 + 1) * px, lanes(t, px)] = (
                    done[q * px : (q + 1) * px]
                )

        loop(slots, cut_away)
        loop(slots, cut_own)
        if it > 0:
            whole_sum(it - 1)
            finish_probe(it - 1)
        loop(slots, lambda t: patch_copy(t).wait_recv())

        def wait_patterns():
            def arrive(i, carry):
                @pl.when(core * half + i != ix)
                def _():
                    pattern_copy(ix, i).wait_recv()

                return carry

            lax.fori_loop(0, half, arrive, 0)

        if it == 0:
            tabs_load.wait()
            for copy in probe_loads:
                copy.wait()
            if runs > 8:
                wait_patterns()

        if runs > 1:
            pg_sum[...] = jnp.zeros_like(pg_sum)

        def run(k):
            first = k * chunk
            spans = [lanes(first // fine_chunk + i, width) for i in range(chunk // fine_chunk)]
            w = jnp.concatenate([wave[...]] * fine_chunk, axis=1)
            psi = [times(w, patches[0, :, span].astype(F32), px) for span in spans]
            for l in range(1, total):
                for i, span in enumerate(spans):
                    phi = both_sides(psi[i], tabs, 0, 1, px, forth)
                    phis[l - 1, :, span] = phi
                    psi[i] = times(phi, patches[l, :, span].astype(F32), px)
            if it == 0 and runs <= 8 and k == 0:
                wait_patterns()
            g = []
            for i in range(len(spans)):
                far = both_sides(psi[i], tabs, 2, 3, px, 1 if it == ITERS - 1 else forth)
                target = []
                for s in range(fine_chunk):
                    t = first + i * fine_chunk + s
                    target.append(pat[t // cap, t % cap].astype(F32))
                target = jnp.concatenate(target, axis=1)
                fr, fi = far[:px], far[px:]
                miss = jnp.where(target >= 0.0, 2.0 * (fr * fr + fi * fi - target), 0.0)
                g.append(jnp.concatenate([miss * fr, miss * fi], axis=0))
            g = [both_sides(one, tabs, 3, 2, px, back) for one in g]
            for l in range(total - 1, -1, -1):
                for i, span in enumerate(spans):
                    before = phis[l - 1, :, span] if l else w
                    grads[l, :, span] = conj_times(before, g[i], px).astype(BF16)
                    g[i] = conj_times(patches[l, :, span].astype(F32), g[i], px)
                    if l:
                        g[i] = both_sides(g[i], tabs, 1, 0, px, back)
            add = None
            for one in g:
                for s in range(fine_chunk):
                    part = one[:, s * px : (s + 1) * px]
                    add = part if add is None else add + part
            if runs == 1:
                pg_mine[it] = add.astype(BF16)
            else:
                pg_sum[...] += add

        if it > 0:
            grad_copy(it - 1).wait_send()
        loop(runs, run)

        if runs > 1:
            pg_mine[it] = pg_sum[...].astype(BF16)
        for d in range(1, plane):
            piece_copy(it, d).start()
        grad_copy(it).start()
        if it == 0:
            loop(slots, build_put)

        def place(source, first, base, c, last):
            def lift(t):
                for q in range(2 * layers):
                    lifted[t, q, pl.ds(rows - px, px), :] = (
                        source[first + q // 2, q % 2 * px : (q % 2 + 1) * px, lanes(t, px)].astype(F32)
                    )

            def spread(t):
                row, _ = slot_corner(t, c)
                for q in range(2 * layers):
                    placed[q, :, lanes(base + t, px)] = lifted[t, q, pl.ds(rows - px - row, rows), :].astype(BF16)

            loop(slots, lift)
            loop(slots, spread)
            span = pl.ds(base * px, slots * px)
            for q in range(2 * layers):
                add = STEP_OBJECT * dot(placed[q, :, span], put_c[span, :])
                for j in range(cols // px):
                    now = field[q, j] - add[:, j * px : (j + 1) * px]
                    if last:
                        obj_out[q // 2, q % 2, :, lanes(j, px)] = now
                    else:
                        field[q, j] = now

        place(grads, core * layers, 0, core, False)
        plane_sum(it)
        grad_copy(it).wait_recv()
        place(g_recv, 0, slots, other, it == ITERS - 1)

    whole_sum(ITERS - 1)
    finish_probe(ITERS - 1)
    probe_out[0] = wave[:px]
    probe_out[1] = wave[px:]

    @pl.when(mine_sends)
    def _():
        for d in range(1, n_tx):
            pattern_copy(along(d)[0], local_s).wait_send()

    loop(slots, lambda t: patch_copy(t).wait_send())
    grad_copy(ITERS - 1).wait_send()
    for it in range(ITERS):
        for d in range(1, plane):
            piece_copy(it, d).wait_send()
        for d in range(1, n_tx):
            zone_copy(it, d).wait_send()
        delta_copy(it).wait_send()


def body(object_field, probe_wave, measured, owner_row, list_rows, list_cols):
    layers, _, rows, cols = object_field.shape
    positions, px, _ = measured.shape
    n_tx, n_ty, n_sl = lax.axis_size("tx"), lax.axis_size("ty"), lax.axis_size("sl")
    cap = list_rows.shape[-1]
    half = n_tx // n_sl
    slots = half * cap
    total = n_sl * layers
    plane = n_ty * n_sl
    deep = 2 * px // n_sl
    tabs = jnp.asarray(real_tables(px))
    tables = [jnp.transpose(one, (0, 3, 1, 2)).reshape(cap, 1, n_tx) for one in (list_rows, list_cols)]
    vmem = pl.BlockSpec(memory_space=pltpu.VMEM)
    anywhere = pl.BlockSpec(memory_space=pl.ANY)
    dma = pltpu.SemaphoreType.DMA
    return pl.pallas_call(
        functools.partial(kernel, n_tx, n_ty, n_sl, cap, positions * n_tx * n_ty),
        out_shape=(
            pltpu.VMEM(object_field.shape, F32),
            pltpu.VMEM(probe_wave.shape, F32),
        ),
        in_specs=[anywhere, anywhere, anywhere, anywhere, anywhere, anywhere, anywhere],
        out_specs=(vmem, vmem),
        scratch_shapes=[
            pltpu.SMEM(tables[0].shape, jnp.int32),
            pltpu.SMEM(tables[1].shape, jnp.int32),
            pltpu.SMEM((1, positions), jnp.int32),
            pltpu.VMEM((2 * layers, cols // px, rows, px), F32),
            pltpu.VMEM(measured.shape, F32),
            pltpu.VMEM(tabs.shape, BF16),
            pltpu.VMEM((half, cap, px, px), BF16),
            pltpu.VMEM((n_tx, cap, px, px), BF16),
            pltpu.VMEM((2 * slots, 2 * px, px), BF16),
            pltpu.VMEM((2 * slots * px, cols), BF16),
            pltpu.VMEM((total, 2 * px, slots * px), BF16),
            pltpu.VMEM((layers, 2 * px, slots * px), BF16),
            pltpu.VMEM((total - 1, 2 * px, slots * px), F32),
            pltpu.VMEM((total, 2 * px, slots * px), BF16),
            pltpu.VMEM((layers, 2 * px, slots * px), BF16),
            pltpu.VMEM((slots, 2 * layers, 2 * rows - px, px), F32),
            pltpu.VMEM((2 * layers, rows, 2 * slots * px), BF16),
            pltpu.VMEM((ITERS, plane, deep, px), BF16),
            pltpu.VMEM((ITERS, 2 * px, px), BF16),
            pltpu.VMEM((ITERS, n_tx, deep, px), BF16),
            pltpu.VMEM((ITERS, 2 * px, px), F32),
            pltpu.VMEM((2 * px, px), F32),
            pltpu.VMEM((2 * px, px), F32),
            dma((2 * layers, cols // px)),
            dma((7,)),
            dma((n_tx,)),
            dma((half,)),
            dma((slots,)),
            dma((slots,)),
            dma((ITERS,)),
            dma((ITERS,)),
            dma((ITERS, plane)),
            dma((ITERS, plane)),
            dma((ITERS, n_tx)),
            dma((ITERS, n_tx)),
            dma((ITERS,)),
            dma((ITERS,)),
        ],
        compiler_params=pltpu.CompilerParams(
            collective_id=0, has_side_effects=True, vmem_limit_bytes=58 * 2**20
        ),
    )(object_field, probe_wave, measured, *tables, owner_row.reshape(1, -1), tabs)


def solution(mesh):
    in_specs = (
        P(("groups", "sl"), None, "tx", "ty"),
        P("groups", None, None),
        P(("groups", "tx", "ty"), None, None),
        P(("groups", "tx", "ty"), None),
        P(("groups", "tx"), "ty", None, None),
        P(("groups", "tx"), "ty", None, None),
    )
    out_specs = (P(("groups", "sl"), None, "tx", "ty"), P("groups", None, None))
    return jax.shard_map(body, mesh=mesh, in_specs=in_specs, out_specs=out_specs, check_vma=False)
```
